32 devices in a mesh: dp: 16 (over z, y, core), tensor: 2 (over x).
Axes of the slice: x: 2, y: 2, z: 4, core: 2. Of those that a mesh axis runs over, the one named last changes fastest.
Arguments:
- tokens: bfloat16 [16384, 1024], P(('dp', 'tensor')), may hold values from -6 to 6
- gain_one: float32 [1024], P(('dp', 'tensor')), may hold values from 0.5 to 1.5
- shift_one: float32 [1024], P(('dp', 'tensor')), may hold values from -2 to 2
- w_qkv: bfloat16 [3, 1024, 1024], P(None, 'dp', 'tensor'), may hold values from -0.1875 to 0.1875
- bias_qv: bfloat16 [2, 16, 64], P(None, 'tensor', 'dp'), may hold values from -2 to 2
- w_out: bfloat16 [1024, 1024], P('tensor', 'dp'), may hold values from -0.5 to 0.5
- bias_out: float32 [1024], P(('dp', 'tensor')), may hold values from -2 to 2
- gain_two: float32 [1024], P(('dp', 'tensor')), may hold values from 0.5 to 1.5
- shift_two: float32 [1024], P(('dp', 'tensor')), may hold values from -2 to 2
- w_up: bfloat16 [1024, 4096], P('dp', 'tensor'), may hold values from -0.1875 to 0.1875
- bias_up: bfloat16 [32, 128], P('tensor', 'dp'), may hold values from -2 to 2
- w_down: bfloat16 [4096, 1024], P('tensor', 'dp'), may hold values from -0.09375 to 0.09375
- bias_down: float32 [1024], P(('dp', 'tensor')), may hold values from -2 to 2
- cotangent: bfloat16 [16384, 1024], P(('dp', 'tensor')), may hold values from -6 to 6
Outputs:
- mixed: bfloat16 [16384, 1024], P(('dp', 'tensor'))
- grad_tokens: bfloat16 [16384, 1024], P(('dp', 'tensor'))
- grad_gain_one: float32 [1024], P(('dp', 'tensor'))
- grad_shift_one: float32 [1024], P(('dp', 'tensor'))
- grad_qkv: float32 [3, 1024, 1024], P(None, 'dp', 'tensor')
- grad_bias_qv: float32 [2, 16, 64], P(None, 'tensor', 'dp')
- grad_out: float32 [1024, 1024], P('tensor', 'dp')
- grad_bias_out: float32 [1024], P(('dp', 'tensor'))
- grad_gain_two: float32 [1024], P(('dp', 'tensor'))
- grad_shift_two: float32 [1024], P(('dp', 'tensor'))
- grad_up: float32 [1024, 4096], P('dp', 'tensor')
- grad_bias_up: float32 [32, 128], P('tensor', 'dp')
- grad_down: float32 [4096, 1024], P('tensor', 'dp')
- grad_bias_down: float32 [1024], P(('dp', 'tensor'))
The draws below stay inside these ranges and needn't reach their ends.
All inputs are finite; a program needn't handle non-finite values.
Results may differ from the reference program's by a relative error of at most 0.019.
Values may be sent and summed in bfloat16 or wider, within the bound.
A program may use at most 192 MiB of HBM per device.

```python
import math
import jax
import jax.numpy as jnp
from jax import lax

D = 1024
H = 16
HD = 64
FF = 4096
TOK_DEV = 512
LENGTH = 1024
TOKENS = 16384
N_DP = 16
N_TENSOR = 2


def with_spikes(drawn, stream_key, source, target, shards_of, factor):
    owner, partner = [(jnp.arange(drawn.shape[dim]) // (drawn.shape[dim] // shards_of)).reshape([-1 if axis == dim else 1 for axis in range(drawn.ndim)]) for dim in (source, target)]
    chosen = jax.random.permutation(stream_key, shards_of)[partner]
    strong = (owner == chosen) | (owner == (partner + shards_of // 2) % shards_of)
    return jnp.where(strong, factor * drawn, drawn)


def level_of(key, extent, shards, least, high):
    def one(position, parts):
        steps = jax.random.uniform(jax.random.fold_in(jax.random.fold_in(key, 6), position), (parts,), jnp.float32, least / len(shards), high / len(shards))
        return jnp.repeat(jnp.exp(steps), extent[position] // parts).reshape((-1,) + (1,) * (len(extent) - position - 1))

    level = one(*shards[0])
    for cut in shards[1:]:
        level = level * one(*cut)
    return level


def normal_values(stream_key, shape, scale, limit, split=(), held_as=jnp.bfloat16):
    drawn = jax.random.normal(stream_key, shape, jnp.float32) * scale
    if len(split) > 0:
        drawn = level_of(stream_key, shape, split, -0.22, 0.18) * drawn
    return jnp.clip(drawn, min=-limit, max=limit).astype(held_as)


def noise_with(key, extent, width, reach, split, heavy, dtype=jnp.bfloat16):
    entries = width * jax.random.normal(key, extent, jnp.float32)
    if split:
        entries = entries * level_of(key, extent, split, -0.22, 0.18)
    return jnp.clip(with_spikes(entries, jax.random.fold_in(key, 3), *heavy), -reach, reach).astype(dtype)


def setup_inputs(seed: int = 0) -> dict:
    key_of = jax.random.split(jax.random.key(seed), 15)
    return {
        "tokens": normal_values(key_of[0], (TOKENS, D), 1.0, 6.0, ((0, 32),)),
        "gain_one": jnp.clip(1.0 + 0.1 * jax.random.normal(key_of[1], (D,), jnp.float32), 0.5, 1.5),
        "shift_one": normal_values(key_of[2], (D,), 0.3, 2.0, ((0, 32),), jnp.float32),
        "w_qkv": normal_values(key_of[3], (3, D, D), D ** -0.5, 0.1875, ((1, 16), (2, 2))),
        "bias_qv": normal_values(key_of[4], (2, H, HD), 0.3, 2.0, ((1, 2), (2, 16))),
        "w_out": normal_values(key_of[5], (D, D), (D // 8) ** -0.5, 0.5, ((0, 2), (1, 16))),
        "bias_out": normal_values(key_of[6], (D,), 0.3, 2.0, ((0, 32),), jnp.float32),
        "gain_two": jnp.clip(1.0 + 0.1 * jax.random.normal(key_of[7], (D,), jnp.float32), 0.5, 1.5),
        "shift_two": normal_values(key_of[8], (D,), 0.3, 2.0, ((0, 32),), jnp.float32),
        "w_up": normal_values(key_of[9], (D, FF), D ** -0.5, 0.1875, ((0, 16), (1, 2))),
        "bias_up": normal_values(key_of[10], (FF // 128, 128), 0.3, 2.0, ((0, 2), (1, 16))),
        "w_down": normal_values(key_of[11], (FF, D), FF ** -0.5, 0.09375, ((0, 2), (1, 16))),
        "bias_down": normal_values(key_of[12], (D,), 0.3, 2.0, ((0, 32),), jnp.float32),
        "cotangent": noise_with(key_of[13], (TOKENS, D), 1.0, 6.0, ((0, 32),), (0, 1, 32, 2.75)),
    }


@jax.custom_vjp
def low(v):
    return lax.optimization_barrier(v.astype(jnp.bfloat16)).astype(jnp.float32)

@jax.custom_vjp
def low_back(v):
    return v

def low_keep(v):
    return (low(v), None)

def low_pass(kept, grad):
    return (grad,)

def back_keep(v):
    return (v, None)

def back_low(kept, grad):
    return (low(grad),)
low.defvjp(low_keep, low_pass)
low_back.defvjp(back_keep, back_low)
EPSILON = 1e-05
MASKED = -1e+30
HIGHEST = lax.Precision.HIGHEST

def matmul(left, right):
    return jnp.dot(left, right, precision=HIGHEST)

def layer_norm(values, gain, shift):
    centred = values - lax.optimization_barrier(jnp.mean(values, axis=-1, keepdims=True))
    inverse = lax.rsqrt(lax.optimization_barrier(jnp.mean(centred * centred, axis=-1, keepdims=True)) + EPSILON)
    return centred * inverse * gain + shift

def head_attend(inputs):
    query, keys, values, slope = inputs
    products = jnp.einsum('sqd,skd->sqk', query, keys, precision=HIGHEST)
    positions = jnp.arange(LENGTH)
    offset = (positions[None, :] - positions[:, None]).astype(jnp.float32)
    scores = low_back(products * (1.0 / math.sqrt(HD)) + slope * offset)
    scores = jnp.where(offset <= 0.0, scores, MASKED)
    row_max = lax.optimization_barrier(jnp.max(scores, axis=-1, keepdims=True))
    exponent = jnp.exp(scores - row_max)
    probs = exponent / lax.optimization_barrier(jnp.sum(exponent, axis=-1, keepdims=True))
    return jnp.einsum('sqk,skd->sqd', low(probs), values, precision=HIGHEST)

def forward(inputs, gain_one, shift_one, w_qkv, bias_qv, w_out, bias_out, gain_two, shift_two, w_up, bias_up, w_down, bias_down):
    rows = inputs.shape[0]
    normed_one = low(layer_norm(inputs, gain_one, shift_one))
    query = low(low_back(matmul(normed_one, w_qkv[0]) + bias_qv[0].reshape(D)))
    keys = low(low_back(matmul(normed_one, w_qkv[1])))
    values = low(low_back(matmul(normed_one, w_qkv[2]) + bias_qv[1].reshape(D)))

    def by_head(tensor):
        return tensor.reshape(rows // LENGTH, LENGTH, H, HD).transpose(2, 0, 1, 3)
    slopes = jnp.exp2(-8.0 * (jnp.arange(H) + 1).astype(jnp.float32) / H)
    attended = lax.map(jax.checkpoint(head_attend), (by_head(query), by_head(keys), by_head(values), slopes))
    attended = low(low_back(attended.transpose(1, 2, 0, 3).reshape(rows, D)))
    middle = inputs + low_back(matmul(attended, w_out)) + bias_out
    normed_two = low(layer_norm(middle, gain_two, shift_two))
    hidden = low_back(matmul(normed_two, w_up) + bias_up.reshape(FF))
    gated = low(jax.nn.gelu(hidden, approximate=True))
    return middle + matmul(gated, w_down) + bias_down

def reference(tokens, gain_one, shift_one, w_qkv, bias_qv, w_out, bias_out, gain_two, shift_two, w_up, bias_up, w_down, bias_down, cotangent):
    params = tuple((item.astype(jnp.float32) for item in (gain_one, shift_one, w_qkv, bias_qv, w_out, bias_out, gain_two, shift_two, w_up, bias_up, w_down, bias_down)))
    group = TOK_DEV * N_TENSOR
    inputs = tokens.astype(jnp.float32).reshape(N_DP, group, D)
    grads_in = cotangent.astype(jnp.float32).reshape(N_DP, group, D)

    def step(totals, pair):
        rows_in, rows_grad = pair
        result, pull = jax.vjp(forward, rows_in, *params)
        grads = pull(rows_grad)
        totals = tuple((total + grad for total, grad in zip(totals, grads[1:])))
        return (totals, (result.astype(jnp.bfloat16), grads[0].astype(jnp.bfloat16)))
    zeros = tuple((jnp.zeros_like(item) for item in params))
    totals, (results, grad_rows) = lax.scan(step, zeros, (inputs, grads_in))
    return (results.reshape(TOKENS, D), grad_rows.reshape(TOKENS, D), totals[0], totals[1], totals[2], totals[3], totals[4], totals[5], totals[6], totals[7], totals[8], totals[9], totals[10], totals[11])
```

```python
import functools
import math

import jax
import jax.numpy as jnp
from jax import lax
from jax.experimental import pallas as pl
from jax.experimental.pallas import tpu as pltpu
from jax.sharding import PartitionSpec as P

H = 16
HD = 64
SEQ_LEN = 1024
PAIR = 2 * HD
QB = 256

EPSILON = 1e-05
MASKED = -1e30
F32 = jnp.float32
BF16 = jnp.bfloat16


def normalize(values):
    centred = values - jnp.mean(values, axis=-1, keepdims=True)
    inverse = lax.rsqrt(jnp.mean(centred * centred, axis=-1, keepdims=True) + EPSILON)
    return (centred * inverse, inverse)


def norm_backward(grad, normed, inverse, gain):
    scaled = grad * gain
    return inverse * (
        scaled
        - jnp.mean(scaled, axis=-1, keepdims=True)
        - normed * jnp.mean(scaled * normed, axis=-1, keepdims=True)
    )


def smooth_gate(values):
    return jax.nn.gelu(values, approximate=True)


def mm(a, b):
    return lax.dot_general(a, b, (((1,), (0,)), ((), ())), preferred_element_type=F32)


def mm_t(a, b):
    return lax.dot_general(a, b, (((1,), (1,)), ((), ())), preferred_element_type=F32)


def t_mm(a, b):
    return lax.dot_general(a, b, (((0,), (0,)), ((), ())), preferred_element_type=F32)


def head_masked(values, head):
    lane = lax.broadcasted_iota(jnp.int32, values.shape, 1)
    return jnp.where(lane // HD == head, values, jnp.zeros_like(values))


def stored_row(flip, position, length):
    half = length // 2
    return pl.multiple_of(((position // half + flip) % 2) * half + position % half, QB)


def attend_kernel(flip_ref, slope_ref, q_ref, k_ref, v_ref, o_ref, k_all, v_all):
    length = q_ref.shape[0]
    half = length // 2
    flip = flip_ref[0]
    first = pl.program_id(1) * 2
    for number in range(2):
        rows = pl.ds(stored_row(flip, number * half, length), half)
        k_all[number * half : (number + 1) * half] = k_ref[rows, :]
        v_all[number * half : (number + 1) * half] = v_ref[rows, :]
    for start in range(0, length, QB):
        end = start + QB
        q = q_ref[pl.ds(stored_row(flip, start, length), QB), :]
        q = (q.astype(F32) * (1.0 / math.sqrt(HD))).astype(BF16)
        offset = (
            lax.broadcasted_iota(jnp.int32, (1, end), 1) - start
        ).astype(F32)
        row = lax.broadcasted_iota(jnp.int32, (QB, QB), 0)
        col = lax.broadcasted_iota(jnp.int32, (QB, QB), 1)
        outs = []
        for head in range(2):
            scores = mm_t(head_masked(q, head), k_all[:end]) + slope_ref[first + head] * offset
            diagonal = jnp.where(col <= row, scores[:, start:], MASKED)
            scores = (
                jnp.concatenate([scores[:, :start], diagonal], axis=1) if start else diagonal
            )
            top = jnp.max(scores, axis=-1, keepdims=True)
            exponent = jnp.exp(scores - top)
            total = jnp.sum(exponent, axis=-1, keepdims=True)
            outs.append(mm(exponent.astype(BF16), v_all[:end]) / total)
        lane = lax.broadcasted_iota(jnp.int32, (QB, PAIR), 1)
        o_ref[pl.ds(stored_row(flip, start, length), QB), :] = jnp.where(
            lane < HD, outs[0], outs[1]
        ).astype(BF16)


def attend_back_kernel(
    flip_ref, slope_ref, q_ref, k_ref, v_ref, g_ref, dq_ref, dk_ref, dv_ref, k_all, v_all, dk, dv
):
    length = q_ref.shape[0]
    half = length // 2
    flip = flip_ref[0]
    first = pl.program_id(1) * 2
    for number in range(2):
        rows = pl.ds(stored_row(flip, number * half, length), half)
        k_all[number * half : (number + 1) * half] = k_ref[rows, :]
        v_all[number * half : (number + 1) * half] = v_ref[rows, :]
    for start in reversed(range(0, length, QB)):
        end = start + QB
        here = pl.ds(stored_row(flip, start, length), QB)
        q = (q_ref[here, :].astype(F32) * (1.0 / math.sqrt(HD))).astype(BF16)
        g = g_ref[here, :]
        offset = (lax.broadcasted_iota(jnp.int32, (end, 1), 0) - start).astype(F32)
        key = lax.broadcasted_iota(jnp.int32, (QB, QB), 0)
        query = lax.broadcasted_iota(jnp.int32, (QB, QB), 1)
        dq_sum = None
        dk_sum = None
        dv_sum = None
        for head in range(2):
            q_head = head_masked(q, head)
            g_head = head_masked(g, head)
            scores = mm_t(k_all[:end], q_head) + slope_ref[first + head] * offset
            diagonal = jnp.where(key <= query, scores[start:], MASKED)
            scores = (
                jnp.concatenate([scores[:start], diagonal], axis=0) if start else diagonal
            )
            top = jnp.max(scores, axis=0, keepdims=True)
            exponent = jnp.exp(scores - top)
            probs = exponent * (1.0 / jnp.sum(exponent, axis=0, keepdims=True))
            grad_probs = mm_t(v_all[:end], g_head)
            inner = jnp.sum(probs * grad_probs, axis=0, keepdims=True)
            grad_scores = (probs * (grad_probs - inner)).astype(BF16)
            dq_part = t_mm(grad_scores, head_masked(k_all[:end], head))
            dk_part = mm(grad_scores, q_head)
            dv_part = mm(probs.astype(BF16), g_head)
            dq_sum = dq_part if dq_sum is None else dq_sum + dq_part
            dk_sum = dk_part if dk_sum is None else dk_sum + dk_part
            dv_sum = dv_part if dv_sum is None else dv_sum + dv_part
        dq_ref[here, :] = (dq_sum * (1.0 / math.sqrt(HD))).astype(BF16)
        if end == length:
            dk[...] = dk_sum
            dv[...] = dv_sum
        else:
            dk[:end] += dk_sum
            dv[:end] += dv_sum
    for number in range(2):
        rows = pl.ds(stored_row(flip, number * half, length), half)
        dk_ref[rows, :] = dk[number * half : (number + 1) * half].astype(BF16)
        dv_ref[rows, :] = dv[number * half : (number + 1) * half].astype(BF16)


def attention_call(kernel, flip, slopes, operands, n_out, scratch, length, costs):
    group, width = operands[0].shape
    block = pl.BlockSpec((length, PAIR), lambda s, h: (s, h))
    scalar = pl.BlockSpec(memory_space=pltpu.SMEM)
    shape = jax.ShapeDtypeStruct((group, width), BF16)
    return pl.pallas_call(
        kernel,
        grid=(group // length, width // PAIR),
        out_shape=[shape] * n_out,
        in_specs=[scalar, scalar] + [block] * len(operands),
        out_specs=[block] * n_out,
        scratch_shapes=scratch,
        compiler_params=pltpu.CompilerParams(vmem_limit_bytes=48 * 1024 * 1024),
        cost_estimate=costs,
    )(flip, slopes, *operands)


def local(
    tokens,
    gain_one,
    shift_one,
    w_qkv,
    bias_qv,
    w_out,
    bias_out,
    gain_two,
    shift_two,
    w_up,
    bias_up,
    w_down,
    bias_down,
    cotangent,
):
    parts = lax.axis_size("tensor")
    n_dp = lax.axis_size("dp")
    everyone = n_dp * parts
    t_index = lax.axis_index("tensor")
    core = lax.axis_index("dp") % 2
    chips = n_dp // 2
    swap_cores = [(i, i ^ 1) for i in range(n_dp)]
    same_core = [list(range(c, n_dp, 2)) for c in range(2)]

    def gather_weight(shard):
        rows, columns = shard.shape
        mine = lax.all_gather(shard, "dp", axis=0, axis_index_groups=same_core, tiled=False)
        theirs = lax.ppermute(mine, "dp", swap_cores)
        first = jnp.where(core == 0, mine, theirs)
        second = jnp.where(core == 0, theirs, mine)
        return jnp.stack([first, second], axis=1).reshape(n_dp * rows, columns)

    def scatter_weight(grad):
        rows, columns = grad.shape
        blocks = grad.reshape(chips, 2, rows // n_dp, columns)
        away = lax.dynamic_index_in_dim(blocks, 1 - core, 1, keepdims=False).astype(BF16)
        keep = lax.dynamic_index_in_dim(blocks, core, 1, keepdims=False).astype(F32)
        both = (keep + lax.ppermute(away, "dp", swap_cores).astype(F32)).astype(BF16)
        both = both.reshape(rows // 2, columns)
        return lax.psum_scatter(
            both, "dp", scatter_dimension=0, axis_index_groups=same_core, tiled=True
        ).astype(F32)

    def gather_rows(mine):
        if parts == 2:
            return [mine, lax.ppermute(mine, "tensor", [(0, 1), (1, 0)])]
        return [lax.all_gather(mine, "tensor", axis=0, tiled=True)]

    def scatter_rows(product, blocks):
        if parts == 2:
            sent = lax.ppermute(product(blocks[1]).astype(BF16), "tensor", [(0, 1), (1, 0)])
            return product(blocks[0]) + sent.astype(F32)
        return lax.psum_scatter(
            product(blocks[0]).astype(BF16), "tensor", scatter_dimension=0, tiled=True
        ).astype(F32)

    def joined(blocks):
        return blocks[0] if len(blocks) == 1 else jnp.concatenate(blocks, axis=0)

    def split(rows):
        if parts == 2:
            return [rows[: rows.shape[0] // 2], rows[rows.shape[0] // 2 :]]
        return [rows]

    vec = gain_one.shape[0]
    n_qv = bias_qv.size
    n_bu = bias_up.size
    packed = jnp.concatenate(
        [gain_one, shift_one, bias_out, gain_two, shift_two, bias_down]
        + [bias_qv.astype(F32).reshape(-1), bias_up.astype(F32).reshape(-1)]
    )
    small = lax.all_gather(packed, ("dp", "tensor"), axis=0, tiled=False)
    gain_a, shift_a, out_shift, gain_b, shift_b, down_shift = (
        small[:, n * vec : (n + 1) * vec].reshape(-1) for n in range(6)
    )
    at = 6 * vec
    local_small = lax.dynamic_index_in_dim(
        small.reshape(n_dp, parts, -1), t_index, 1, keepdims=False
    )
    local_heads = bias_qv.shape[1]
    width = local_heads * HD
    qv_shift = (
        local_small[:, at : at + n_qv]
        .reshape(n_dp, 2, local_heads, -1)
        .transpose(1, 2, 0, 3)
        .reshape(2, width)
    )
    up_shift = (
        local_small[:, at + n_qv :]
        .reshape(n_dp, bias_up.shape[0], -1)
        .transpose(1, 0, 2)
        .reshape(-1)
    )
    hidden_units = up_shift.shape[0]

    first_full = gather_weight(
        jnp.concatenate([w_qkv[0], w_qkv[1], w_qkv[2], w_out.T], axis=1)
    )
    up_full = gather_weight(w_up)
    down_t = gather_weight(w_down.T)
    qkv_full = first_full[:, : 3 * width]
    out_t = first_full[:, 3 * width :]

    rows = tokens.shape[0]
    group = rows * parts
    length = min(SEQ_LEN, group)
    sequences = group // length
    head_ids = t_index * local_heads + lax.iota(jnp.int32, local_heads)
    slopes = jnp.exp2(-8.0 * (head_ids + 1).astype(F32) / H)
    flip = (t_index if parts == 2 else 0 * t_index).astype(jnp.int32).reshape(1)

    cot_blocks = gather_rows(cotangent)
    inputs = tokens.astype(F32)
    normed_one, inverse_one = normalize(inputs)
    one_blocks = gather_rows((normed_one * gain_a + shift_a).astype(BF16))
    qkv_shift = jnp.concatenate([qv_shift[0], jnp.zeros((width,), F32), qv_shift[1]])
    qkv_low = joined([(mm(b, qkv_full) + qkv_shift).astype(BF16) for b in one_blocks])
    query, keys, values = (qkv_low[:, n * width : (n + 1) * width] for n in range(3))
    pair_area = sequences * local_heads * length * length
    vmem = pltpu.VMEM((length, PAIR), BF16)
    (attended,) = attention_call(
        attend_kernel,
        flip,
        slopes,
        (query, keys, values),
        1,
        [vmem, vmem],
        length,
        pl.CostEstimate(
            flops=4 * PAIR * pair_area, bytes_accessed=8 * group * width, transcendentals=pair_area
        ),
    )
    middle = (
        inputs + scatter_rows(lambda b: mm_t(b, out_t), split(attended)) + out_shift
    )
    normed_two, inverse_two = normalize(middle)
    two_blocks = gather_rows((normed_two * gain_b + shift_b).astype(BF16))
    hidden = [mm(b, up_full) + up_shift for b in two_blocks]
    gated = [smooth_gate(h).astype(BF16) for h in hidden]
    grad_gated = [mm(c, down_t) for c in cot_blocks]
    grad_hidden = [
        jax.vjp(smooth_gate, h)[1](g)[0].astype(BF16) for h, g in zip(hidden, grad_gated)
    ]
    grad_two = scatter_rows(lambda b: mm_t(b, up_full), grad_hidden)
    output = middle + scatter_rows(lambda b: mm_t(b, down_t), gated) + down_shift

    cot_all = joined(cot_blocks)
    grad_hidden_all = joined(grad_hidden)
    summed_down = scatter_weight(t_mm(cot_all, joined(gated)).astype(BF16))
    summed_up = scatter_weight(t_mm(joined(two_blocks), grad_hidden_all).astype(BF16))
    grad_up_shift = jnp.sum(grad_hidden_all.astype(F32), axis=0)

    grad_out_rows = cotangent.astype(F32)
    grad_down_shift = jnp.sum(grad_out_rows, axis=0)
    grad_gain_b = jnp.sum(grad_two * normed_two, axis=0)
    grad_shift_b = jnp.sum(grad_two, axis=0)
    grad_middle = grad_out_rows + norm_backward(grad_two, normed_two, inverse_two, gain_b)
    grad_out_shift = jnp.sum(grad_middle, axis=0)
    low_blocks = gather_rows(grad_middle.astype(BF16))
    grad_attended = joined([mm(b, out_t).astype(BF16) for b in low_blocks])
    scratch = [vmem, vmem] + [pltpu.VMEM((length, PAIR), F32)] * 2
    grad_qkv_parts = attention_call(
        attend_back_kernel,
        flip,
        slopes,
        (query, keys, values, grad_attended),
        3,
        scratch,
        length,
        pl.CostEstimate(
            flops=10 * PAIR * pair_area,
            bytes_accessed=14 * group * width,
            transcendentals=pair_area,
        ),
    )
    grad_qkv_rows = jnp.concatenate(grad_qkv_parts, axis=1)
    grad_one = scatter_rows(lambda b: mm_t(b, qkv_full), split(grad_qkv_rows))
    grad_first = jnp.concatenate(
        [
            t_mm(joined(one_blocks), grad_qkv_rows).astype(BF16),
            t_mm(joined(low_blocks), attended).astype(BF16),
        ],
        axis=1,
    )
    summed_first = scatter_weight(grad_first)
    grad_qv_shift = jnp.stack(
        [
            jnp.sum(grad_qkv_parts[0].astype(F32), axis=0),
            jnp.sum(grad_qkv_parts[2].astype(F32), axis=0),
        ]
    )
    grad_gain_a = jnp.sum(grad_one * normed_one, axis=0)
    grad_shift_a = jnp.sum(grad_one, axis=0)
    grad_inputs = grad_middle + norm_backward(grad_one, normed_one, inverse_one, gain_a)

    mine = (lax.iota(jnp.int32, parts) == t_index)[None, :, None]

    def placed(values):
        return jnp.where(mine, values.reshape(n_dp, 1, -1), 0.0).reshape(everyone, -1)

    packed_grads = jnp.concatenate(
        [
            v.reshape(everyone, vec)
            for v in (
                grad_gain_a,
                grad_shift_a,
                grad_out_shift,
                grad_gain_b,
                grad_shift_b,
                grad_down_shift,
            )
        ]
        + [
            placed(grad_qv_shift.reshape(2, local_heads, n_dp, -1).transpose(2, 0, 1, 3)),
            placed(grad_up_shift.reshape(bias_up.shape[0], n_dp, -1).transpose(1, 0, 2)),
        ],
        axis=1,
    )
    sums = lax.psum_scatter(
        packed_grads, ("dp", "tensor"), scatter_dimension=0, tiled=True
    ).reshape(-1)
    sum_gain_a, sum_shift_a, sum_out_shift, sum_gain_b, sum_shift_b, sum_down_shift = (
        sums[n * vec : (n + 1) * vec] for n in range(6)
    )
    summed_qkv = jnp.stack([summed_first[:, n * width : (n + 1) * width] for n in range(3)])
    return (
        output.astype(BF16),
        grad_inputs.astype(BF16),
        sum_gain_a,
        sum_shift_a,
        summed_qkv,
        sums[at : at + n_qv].reshape(bias_qv.shape),
        summed_first[:, 3 * width :].T,
        sum_out_shift,
        sum_gain_b,
        sum_shift_b,
        summed_up,
        sums[at + n_qv :].reshape(bias_up.shape),
        summed_down.T,
        sum_down_shift,
    )


def solution(mesh):
    return jax.shard_map(
        local,
        mesh=mesh,
        in_specs=(
            P(("dp", "tensor"), None),
            P(("dp", "tensor")),
            P(("dp", "tensor")),
            P(None, "dp", "tensor"),
            P(None, "tensor", "dp"),
            P("tensor", "dp"),
            P(("dp", "tensor")),
            P(("dp", "tensor")),
            P(("dp", "tensor")),
            P("dp", "tensor"),
            P("tensor", "dp"),
            P("tensor", "dp"),
            P(("dp", "tensor")),
            P(("dp", "tensor"), None),
        ),
        out_specs=(
            P(("dp", "tensor"), None),
            P(("dp", "tensor"), None),
            P(("dp", "tensor")),
            P(("dp", "tensor")),
            P(None, "dp", "tensor"),
            P(None, "tensor", "dp"),
            P("tensor", "dp"),
            P(("dp", "tensor")),
            P(("dp", "tensor")),
            P(("dp", "tensor")),
            P("dp", "tensor"),
            P("tensor", "dp"),
            P("tensor", "dp"),
            P(("dp", "tensor")),
        ),
        check_vma=False,
    )
```

```python
import functools
import math

import jax
import jax.numpy as jnp
from jax import lax
from jax.experimental import pallas as pl
from jax.experimental.pallas import tpu as pltpu
from jax.sharding import PartitionSpec as P

H = 16
HD = 64
SEQ_LEN = 1024
PAIR = 2 * HD
QB = 256

EPSILON = 1e-05
MASKED = -1e30
F32 = jnp.float32
BF16 = jnp.bfloat16


def normalize(values):
    centred = values - jnp.mean(values, axis=-1, keepdims=True)
    inverse = lax.rsqrt(jnp.mean(centred * centred, axis=-1, keepdims=True) + EPSILON)
    return (centred * inverse, inverse)


def norm_backward(grad, normed, inverse, gain):
    scaled = grad * gain
    return inverse * (
        scaled
        - jnp.mean(scaled, axis=-1, keepdims=True)
        - normed * jnp.mean(scaled * normed, axis=-1, keepdims=True)
    )


def smooth_gate(values):
    return jax.nn.gelu(values, approximate=True)


def mm(a, b):
    return lax.dot_general(a, b, (((1,), (0,)), ((), ())), preferred_element_type=F32)


def mm_t(a, b):
    return lax.dot_general(a, b, (((1,), (1,)), ((), ())), preferred_element_type=F32)


def t_mm(a, b):
    return lax.dot_general(a, b, (((0,), (0,)), ((), ())), preferred_element_type=F32)


def head_masked(values, head):
    lane = lax.broadcasted_iota(jnp.int32, values.shape, 1)
    return jnp.where(lane // HD == head, values, jnp.zeros_like(values))


def stored_row(flip, position, length):
    half = length // 2
    return pl.multiple_of(((position // half + flip) % 2) * half + position % half, QB)


def attend_kernel(flip_ref, slope_ref, q_ref, k_ref, v_ref, o_ref, k_all, v_all):
    length = q_ref.shape[0]
    half = length // 2
    flip = flip_ref[0]
    first = pl.program_id(1) * 2
    for number in range(2):
        rows = pl.ds(stored_row(flip, number * half, length), half)
        k_all[number * half : (number + 1) * half] = k_ref[rows, :]
        v_all[number * half : (number + 1) * half] = v_ref[rows, :]
    for start in range(0, length, QB):
        end = start + QB
        q = q_ref[pl.ds(stored_row(flip, start, length), QB), :]
        q = (q.astype(F32) * (1.0 / math.sqrt(HD))).astype(BF16)
        offset = (
            lax.broadcasted_iota(jnp.int32, (1, end), 1) - start
        ).astype(F32)
        row = lax.broadcasted_iota(jnp.int32, (QB, QB), 0)
        col = lax.broadcasted_iota(jnp.int32, (QB, QB), 1)
        outs = []
        for head in range(2):
            scores = mm_t(head_masked(q, head), k_all[:end]) + slope_ref[first + head] * offset
            diagonal = jnp.where(col <= row, scores[:, start:], MASKED)
            scores = (
                jnp.concatenate([scores[:, :start], diagonal], axis=1) if start else diagonal
            )
            top = jnp.max(scores, axis=-1, keepdims=True)
            exponent = jnp.exp(scores - top)
            total = jnp.sum(exponent, axis=-1, keepdims=True)
            outs.append(mm(exponent.astype(BF16), v_all[:end]) / total)
        lane = lax.broadcasted_iota(jnp.int32, (QB, PAIR), 1)
        o_ref[pl.ds(stored_row(flip, start, length), QB), :] = jnp.where(
            lane < HD, outs[0], outs[1]
        ).astype(BF16)


def attend_back_kernel(
    flip_ref, slope_ref, q_ref, k_ref, v_ref, g_ref, dq_ref, dk_ref, dv_ref, k_all, v_all, dk, dv
):
    length = q_ref.shape[0]
    half = length // 2
    flip = flip_ref[0]
    first = pl.program_id(1) * 2
    for number in range(2):
        rows = pl.ds(stored_row(flip, number * half, length), half)
        k_all[number * half : (number + 1) * half] = k_ref[rows, :]
        v_all[number * half : (number + 1) * half] = v_ref[rows, :]
    for start in reversed(range(0, length, QB)):
        end = start + QB
        here = pl.ds(stored_row(flip, start, length), QB)
        q = (q_ref[here, :].astype(F32) * (1.0 / math.sqrt(HD))).astype(BF16)
        g = g_ref[here, :]
        offset = (lax.broadcasted_iota(jnp.int32, (end, 1), 0) - start).astype(F32)
        key = lax.broadcasted_iota(jnp.int32, (QB, QB), 0)
        query = lax.broadcasted_iota(jnp.int32, (QB, QB), 1)
        dq_sum = None
        dk_sum = None
        dv_sum = None
        for head in range(2):
            q_head = head_masked(q, head)
            g_head = head_masked(g, head)
            scores = mm_t(k_all[:end], q_head) + slope_ref[first + head] * offset
            diagonal = jnp.where(key <= query, scores[start:], MASKED)
            scores = (
                jnp.concatenate([scores[:start], diagonal], axis=0) if start else diagonal
            )
            top = jnp.max(scores, axis=0, keepdims=True)
            exponent = jnp.exp(scores - top)
            probs = exponent * (1.0 / jnp.sum(exponent, axis=0, keepdims=True))
            grad_probs = mm_t(v_all[:end], g_head)
            inner = jnp.sum(probs * grad_probs, axis=0, keepdims=True)
            grad_scores = (probs * (grad_probs - inner)).astype(BF16)
            dq_part = t_mm(grad_scores, head_masked(k_all[:end], head))
            dk_part = mm(grad_scores, q_head)
            dv_part = mm(probs.astype(BF16), g_head)
            dq_sum = dq_part if dq_sum is None else dq_sum + dq_part
            dk_sum = dk_part if dk_sum is None else dk_sum + dk_part
            dv_sum = dv_part if dv_sum is None else dv_sum + dv_part
        dq_ref[here, :] = (dq_sum * (1.0 / math.sqrt(HD))).astype(BF16)
        if end == length:
            dk[...] = dk_sum
            dv[...] = dv_sum
        else:
            dk[:end] += dk_sum
            dv[:end] += dv_sum
    for number in range(2):
        rows = pl.ds(stored_row(flip, number * half, length), half)
        dk_ref[rows, :] = dk[number * half : (number + 1) * half].astype(BF16)
        dv_ref[rows, :] = dv[number * half : (number + 1) * half].astype(BF16)


def attention_call(kernel, flip, slopes, operands, n_out, scratch, length, costs):
    group, width = operands[0].shape
    block = pl.BlockSpec((length, PAIR), lambda s, h: (s, h))
    scalar = pl.BlockSpec(memory_space=pltpu.SMEM)
    shape = jax.ShapeDtypeStruct((group, width), BF16)
    return pl.pallas_call(
        kernel,
        grid=(group // length, width // PAIR),
        out_shape=[shape] * n_out,
        in_specs=[scalar, scalar] + [block] * len(operands),
        out_specs=[block] * n_out,
        scratch_shapes=scratch,
        compiler_params=pltpu.CompilerParams(vmem_limit_bytes=48 * 1024 * 1024),
        cost_estimate=costs,
    )(flip, slopes, *operands)


def ring_place(chip, chips):
    return chip // 2 + (chip % 2) * (chips - 1 - 2 * (chip // 2))


def ring_chip(place, chips):
    place = lax.rem(place + 2 * chips, chips)
    far = place // (chips // 2)
    return far * (2 * (chips - 1 - place) + 1) + (1 - far) * 2 * place


def remote(src, dst, send, recv, device):
    return pltpu.make_async_remote_copy(
        src_ref=src,
        dst_ref=dst,
        send_sem=send,
        recv_sem=recv,
        device_id=device,
        device_id_type=pl.DeviceIdType.MESH,
    )


def greet(devices):
    barrier = pltpu.get_barrier_semaphore()
    for device in devices:
        pl.semaphore_signal(barrier, inc=1, device_id=device, device_id_type=pl.DeviceIdType.MESH)
    pl.semaphore_wait(barrier, len(devices))


def neighbours(chips, parts):
    index = lax.axis_index("dp")
    tensor = lax.axis_index("tensor")
    core = lax.rem(index, 2)
    place = ring_place(index // 2, chips)
    right = (ring_chip(place + 1, chips) * 2 + core, tensor)
    left = (ring_chip(place - 1, chips) * 2 + core, tensor)
    twin = (index + 1 - 2 * core, tensor)
    peers = [(index, lax.rem(tensor + k, parts)) for k in range(1, parts)]
    return core, place, tensor, right, left, twin, peers


def gather_kernel(chips, parts, *refs):
    pair = parts == 2
    if pair:
        x_ref, small_ref, tok_ref, full_ref, all_ref, other_ref = refs[:6]
        sems = refs[6:]
    else:
        x_ref, small_ref, full_ref, all_ref = refs[:4]
        sems = refs[4:]
    here_sem, big_s, big_r, swap_s, swap_r, sm_s, sm_r, smw_s, smw_r, ten_s, ten_r, tok_s, tok_r = sems
    core, place, tensor, right, left, twin, peers = neighbours(chips, parts)
    mine = ring_chip(place, chips)
    steps = chips // 2
    half = x_ref.shape[0] // 2
    greet([right, left, twin] + peers)
    waits = []
    if pair:
        tok = remote(tok_ref, other_ref, tok_s.at[0], tok_r.at[0], peers[0])
        tok.start()
    here = pltpu.make_async_copy(x_ref, full_ref.at[mine, core], here_sem.at[0])
    here.start()
    here_small = pltpu.make_async_copy(small_ref, all_ref.at[tensor, mine, core], here_sem.at[1])
    here_small.start()
    swaps = []
    small_swaps = []

    def swap(chip, first):
        n = len(swaps)
        small_src = small_ref if first else all_ref.at[tensor, chip, core]
        copy = remote(small_src, all_ref.at[tensor, chip, core], smw_s.at[n], smw_r.at[n], twin)
        copy.start()
        small_swaps.append(copy)
        src = x_ref if first else full_ref.at[chip, core]
        copy = remote(src, full_ref.at[chip, core], swap_s.at[n], swap_r.at[n], twin)
        copy.start()
        swaps.append(copy)

    previous = []
    for step in range(steps):
        started = []
        for copy in previous:
            copy.wait_recv()
        for side, device in ((0, right), (1, left)):
            chip = ring_chip(place - step if side == 0 else place + step, chips)
            slot = side * steps + step
            if step < steps - 1 or side == 0:
                src = small_ref if step == 0 else all_ref.at[tensor, chip, core]
                copy = remote(
                    src, all_ref.at[tensor, chip, core], sm_s.at[slot], sm_r.at[slot], device
                )
                copy.start()
                started.append(copy)
            src = x_ref if step == 0 else full_ref.at[chip, core]
            dst = full_ref.at[chip, core]
            if step == steps - 1:
                rows = pl.ds(side * half, half)
                src, dst = src.at[rows], dst.at[rows]
            copy = remote(src, dst, big_s.at[slot], big_r.at[slot], device)
            copy.start()
            started.append(copy)
        if step == 0:
            swap(mine, True)
        else:
            swap(ring_chip(place - step, chips), False)
            swap(ring_chip(place + step, chips), False)
        waits += started
        previous = started
    for copy in previous:
        copy.wait_recv()
    swap(ring_chip(place + steps, chips), False)
    here_small.wait()
    for copy in small_swaps:
        copy.wait_recv()
    spread = []
    for k, peer in enumerate(peers):
        copy = remote(all_ref.at[tensor], all_ref.at[tensor], ten_s.at[k], ten_r.at[k], peer)
        copy.start()
        spread.append(copy)
    here.wait()
    for copy in swaps:
        copy.wait_recv()
    for copy in waits + swaps + small_swaps:
        copy.wait_send()
    for copy in spread:
        copy.wait()
    if pair:
        tok.wait()


def gather_call(shard, small, tokens, chips, parts):
    rows, columns = shard.shape
    anywhere = pl.BlockSpec(memory_space=pl.ANY)
    out = [
        jax.ShapeDtypeStruct((chips, 2, rows, columns), BF16),
        jax.ShapeDtypeStruct((parts, chips, 2) + small.shape, F32),
    ]
    operands = [shard, small]
    if parts == 2:
        out.append(jax.ShapeDtypeStruct(tokens.shape, BF16))
        operands.append(tokens)
    sem = pltpu.SemaphoreType.DMA
    result = pl.pallas_call(
        functools.partial(gather_kernel, chips, parts),
        out_shape=out,
        in_specs=[anywhere] * len(operands),
        out_specs=[anywhere] * len(out),
        scratch_shapes=[sem((2,))]
        + [sem((chips,))] * 8
        + [sem((parts - 1,))] * 2
        + [sem((1,))] * 2,
        compiler_params=pltpu.CompilerParams(collective_id=0, has_side_effects=True),
        cost_estimate=pl.CostEstimate(
            flops=0, bytes_accessed=64 * rows * columns, transcendentals=0
        ),
    )(*operands)
    return list(result) + [None] * (3 - len(out))


def reduce_kernel(chips, parts, g_ref, s_ref, o_ref, so_ref, *scratch):
    (pair_in, ring_in, ring_out, sm_ten, sm_sum, sm_pair, sm_in, sm_out) = scratch[:8]
    pair_s, pair_r, big_s, big_r, ten_s, ten_r, smp_s, smp_r, sm_s, sm_r = scratch[8:]
    core, place, tensor, right, left, twin, peers = neighbours(chips, parts)
    steps = chips // 2
    half = g_ref.shape[2] // 2
    greet([right, left, twin] + peers)
    order = [steps]
    for n in reversed(range(1, steps)):
        order += [-n, n]
    order.append(0)
    away = 1 - core
    done = []
    ten = []
    for k, peer in enumerate(peers):
        goal = lax.rem(tensor + k + 1, parts)
        copy = remote(s_ref.at[goal], sm_ten.at[k], ten_s.at[k], ten_r.at[k], peer)
        copy.start()
        ten.append(copy)
    pairs = {}
    for n, shift in enumerate(order):
        chip = ring_chip(place + shift, chips)
        copy = remote(g_ref.at[chip, away], pair_in.at[n], pair_s.at[n], pair_r.at[n], twin)
        copy.start()
        pairs[shift] = (n, copy)

    def own(shift):
        n, copy = pairs[shift]
        if shift not in done:
            copy.wait_recv()
            done.append(shift)
        chip = ring_chip(place + shift, chips)
        return g_ref[chip, core].astype(F32) + pair_in[n].astype(F32)

    for copy in ten:
        copy.wait_recv()
    total = s_ref[tensor]
    for k in range(len(peers)):
        total = total + sm_ten[k]
    sm_sum[...] = total
    sm_pair_copy = remote(sm_sum.at[away], sm_pair, smp_s.at[0], smp_r.at[0], twin)
    sm_pair_copy.start()
    sends = list(ten)
    arrived = {}
    for step in range(steps):
        for side, device in ((0, left), (1, right)):
            shift = (step - steps) if side == 0 else (steps - step)
            slot = side * steps + step
            if step == 0:
                rows = pl.ds(side * half, half)
                ring_out[slot] = own(steps).astype(BF16)
                copy = remote(
                    ring_out.at[slot, rows],
                    ring_in.at[slot, rows],
                    big_s.at[slot],
                    big_r.at[slot],
                    device,
                )
            else:
                value = own(shift)
                arrived[side].wait_recv()
                if step == 1:
                    rows = slice(side * half, (side + 1) * half)
                    rest = slice((1 - side) * half, (2 - side) * half)
                    ring_out[slot, rows] = (
                        value[rows] + ring_in[slot - 1, rows].astype(F32)
                    ).astype(BF16)
                    ring_out[slot, rest] = value[rest].astype(BF16)
                else:
                    ring_out[slot] = (value + ring_in[slot - 1].astype(F32)).astype(BF16)
                copy = remote(
                    ring_out.at[slot], ring_in.at[slot], big_s.at[slot], big_r.at[slot], device
                )
            copy.start()
            arrived[side] = copy
            sends.append(copy)
    sm_pair_copy.wait_recv()
    kept = {}
    small_arrived = {}

    def own_small(shift):
        chip = ring_chip(place + shift, chips)
        return sm_sum[core, chip] + sm_pair[chip]

    for step in range(steps):
        for side, device in ((0, left), (1, right)):
            if step == 0 and side == 1:
                continue
            shift = (step - steps) if side == 0 else (steps - step)
            slot = side * steps + step
            value = own_small(shift)
            if side in small_arrived:
                small_arrived[side].wait_recv()
                value = value + sm_in[slot - 1]
            sm_out[slot] = value
            copy = remote(sm_out.at[slot], sm_in.at[slot], sm_s.at[slot], sm_r.at[slot], device)
            copy.start()
            small_arrived[side] = copy
            sends.append(copy)
    value = own(0)
    for side in range(2):
        arrived[side].wait_recv()
        value = value + ring_in[(side + 1) * steps - 1].astype(F32)
    o_ref[...] = value
    value = own_small(0)
    for side in range(2):
        small_arrived[side].wait_recv()
        value = value + sm_in[(side + 1) * steps - 1]
    so_ref[...] = value
    for _, copy in pairs.values():
        copy.wait_send()
    sm_pair_copy.wait_send()
    for copy in sends:
        copy.wait_send()


def reduce_call(grad, small, chips, parts):
    rows, columns = grad.shape[2:]
    tile = small.shape[3:]
    sem = pltpu.SemaphoreType.DMA
    vmem = pl.BlockSpec(memory_space=pltpu.VMEM)
    return pl.pallas_call(
        functools.partial(reduce_kernel, chips, parts),
        out_shape=[
            jax.ShapeDtypeStruct((rows, columns), F32),
            jax.ShapeDtypeStruct(tile, F32),
        ],
        in_specs=[vmem, vmem],
        out_specs=[vmem, vmem],
        scratch_shapes=[
            pltpu.VMEM((chips, rows, columns), BF16),
            pltpu.VMEM((chips, rows, columns), BF16),
            pltpu.VMEM((chips, rows, columns), BF16),
            pltpu.VMEM((parts - 1, 2, chips) + tile, F32),
            pltpu.VMEM((2, chips) + tile, F32),
            pltpu.VMEM((chips,) + tile, F32),
            pltpu.VMEM((chips,) + tile, F32),
            pltpu.VMEM((chips,) + tile, F32),
        ]
        + [sem((chips,))] * 4
        + [sem((parts - 1,))] * 2
        + [sem((1,))] * 2
        + [sem((chips,))] * 2,
        compiler_params=pltpu.CompilerParams(
            collective_id=1, has_side_effects=True, vmem_limit_bytes=40 * 1024 * 1024
        ),
        cost_estimate=pl.CostEstimate(
            flops=0, bytes_accessed=64 * rows * columns, transcendentals=0
        ),
    )(grad, small)


def local(
    tokens,
    gain_one,
    shift_one,
    w_qkv,
    bias_qv,
    w_out,
    bias_out,
    gain_two,
    shift_two,
    w_up,
    bias_up,
    w_down,
    bias_down,
    cotangent,
):
    parts = lax.axis_size("tensor")
    n_dp = lax.axis_size("dp")
    everyone = n_dp * parts
    t_index = lax.axis_index("tensor")
    chips = n_dp // 2

    def gather_weight(shard):
        return lax.all_gather(shard, "dp", axis=0, tiled=True)

    def scatter_weight(grad):
        return lax.psum_scatter(grad, "dp", scatter_dimension=0, tiled=True).astype(F32)

    def gather_rows(mine):
        if parts == 2:
            return [mine, lax.ppermute(mine, "tensor", [(0, 1), (1, 0)])]
        return [lax.all_gather(mine, "tensor", axis=0, tiled=True)]

    def scatter_rows(product, blocks):
        if parts == 2:
            sent = lax.ppermute(product(blocks[1]).astype(BF16), "tensor", [(0, 1), (1, 0)])
            return product(blocks[0]) + sent.astype(F32)
        return lax.psum_scatter(
            product(blocks[0]).astype(BF16), "tensor", scatter_dimension=0, tiled=True
        ).astype(F32)

    def joined(blocks):
        return blocks[0] if len(blocks) == 1 else jnp.concatenate(blocks, axis=0)

    def split(rows):
        if parts == 2:
            return [rows[: rows.shape[0] // 2], rows[rows.shape[0] // 2 :]]
        return [rows]

    vec = gain_one.shape[0]
    n_qv = bias_qv.size
    n_bu = bias_up.size
    packed = jnp.concatenate(
        [gain_one, shift_one, bias_out, gain_two, shift_two, bias_down]
        + [bias_qv.astype(F32).reshape(-1), bias_up.astype(F32).reshape(-1)]
    )
    tile = (8, 128)
    pad = tile[0] * tile[1] - packed.size
    first_shard = jnp.concatenate([w_qkv[0], w_qkv[1], w_qkv[2], w_out.T], axis=1)
    first_full, small, other_tokens = gather_call(
        first_shard, jnp.pad(packed, (0, pad)).reshape(tile), tokens, chips, parts
    )
    first_full = first_full.reshape(-1, first_shard.shape[1])
    small = small.reshape(parts, n_dp, -1).transpose(1, 0, 2).reshape(everyone, -1)
    gain_a, shift_a, out_shift, gain_b, shift_b, down_shift = (
        small[:, n * vec : (n + 1) * vec].reshape(-1) for n in range(6)
    )
    at = 6 * vec
    end = at + n_qv + n_bu
    local_small = lax.dynamic_index_in_dim(
        small.reshape(n_dp, parts, -1), t_index, 1, keepdims=False
    )
    local_heads = bias_qv.shape[1]
    width = local_heads * HD
    qv_shift = (
        local_small[:, at : at + n_qv]
        .reshape(n_dp, 2, local_heads, -1)
        .transpose(1, 2, 0, 3)
        .reshape(2, width)
    )
    up_shift = (
        local_small[:, at + n_qv : end]
        .reshape(n_dp, bias_up.shape[0], -1)
        .transpose(1, 0, 2)
        .reshape(-1)
    )
    hidden_units = up_shift.shape[0]

    up_full = gather_weight(w_up)
    down_t = gather_weight(w_down.T)
    qkv_full = first_full[:, : 3 * width]
    out_t = first_full[:, 3 * width :]

    rows = tokens.shape[0]
    group = rows * parts
    length = min(SEQ_LEN, group)
    sequences = group // length
    head_ids = t_index * local_heads + lax.iota(jnp.int32, local_heads)
    slopes = jnp.exp2(-8.0 * (head_ids + 1).astype(F32) / H)
    flip = (t_index if parts == 2 else 0 * t_index).astype(jnp.int32).reshape(1)

    cot_blocks = gather_rows(cotangent)
    inputs = tokens.astype(F32)
    normed_one, inverse_one = normalize(inputs)
    low_one = (normed_one * gain_a + shift_a).astype(BF16)
    if parts == 2:
        other_normed = normalize(other_tokens.astype(F32))[0]
        one_blocks = [low_one, (other_normed * gain_a + shift_a).astype(BF16)]
    else:
        one_blocks = gather_rows(low_one)
    qkv_shift = jnp.concatenate([qv_shift[0], jnp.zeros((width,), F32), qv_shift[1]])
    qkv_low = joined([(mm(b, qkv_full) + qkv_shift).astype(BF16) for b in one_blocks])
    query, keys, values = (qkv_low[:, n * width : (n + 1) * width] for n in range(3))
    pair_area = sequences * local_heads * length * length
    vmem = pltpu.VMEM((length, PAIR), BF16)
    (attended,) = attention_call(
        attend_kernel,
        flip,
        slopes,
        (query, keys, values),
        1,
        [vmem, vmem],
        length,
        pl.CostEstimate(
            flops=4 * PAIR * pair_area, bytes_accessed=8 * group * width, transcendentals=pair_area
        ),
    )
    middle = (
        inputs + scatter_rows(lambda b: mm_t(b, out_t), split(attended)) + out_shift
    )
    normed_two, inverse_two = normalize(middle)
    two_blocks = gather_rows((normed_two * gain_b + shift_b).astype(BF16))
    hidden = [mm(b, up_full) + up_shift for b in two_blocks]
    gated = [smooth_gate(h).astype(BF16) for h in hidden]
    grad_gated = [mm(c, down_t) for c in cot_blocks]
    grad_hidden = [
        jax.vjp(smooth_gate, h)[1](g)[0].astype(BF16) for h, g in zip(hidden, grad_gated)
    ]
    grad_two = scatter_rows(lambda b: mm_t(b, up_full), grad_hidden)
    output = middle + scatter_rows(lambda b: mm_t(b, down_t), gated) + down_shift

    cot_all = joined(cot_blocks)
    grad_hidden_all = joined(grad_hidden)
    summed_down = scatter_weight(t_mm(cot_all, joined(gated)).astype(BF16))
    summed_up = scatter_weight(t_mm(joined(two_blocks), grad_hidden_all).astype(BF16))
    grad_up_shift = jnp.sum(grad_hidden_all.astype(F32), axis=0)

    grad_out_rows = cotangent.astype(F32)
    grad_down_shift = jnp.sum(grad_out_rows, axis=0)
    grad_gain_b = jnp.sum(grad_two * normed_two, axis=0)
    grad_shift_b = jnp.sum(grad_two, axis=0)
    grad_middle = grad_out_rows + norm_backward(grad_two, normed_two, inverse_two, gain_b)
    grad_out_shift = jnp.sum(grad_middle, axis=0)
    low_blocks = gather_rows(grad_middle.astype(BF16))
    grad_attended = joined([mm(b, out_t).astype(BF16) for b in low_blocks])
    scratch = [vmem, vmem] + [pltpu.VMEM((length, PAIR), F32)] * 2
    grad_qkv_parts = attention_call(
        attend_back_kernel,
        flip,
        slopes,
        (query, keys, values, grad_attended),
        3,
        scratch,
        length,
        pl.CostEstimate(
            flops=10 * PAIR * pair_area,
            bytes_accessed=14 * group * width,
            transcendentals=pair_area,
        ),
    )
    grad_qkv_rows = jnp.concatenate(grad_qkv_parts, axis=1)
    grad_one = scatter_rows(lambda b: mm_t(b, qkv_full), split(grad_qkv_rows))
    grad_first = jnp.concatenate(
        [
            t_mm(joined(one_blocks), grad_qkv_rows).astype(BF16),
            t_mm(joined(low_blocks), attended).astype(BF16),
        ],
        axis=1,
    )
    grad_qv_shift = jnp.stack(
        [
            jnp.sum(grad_qkv_parts[0].astype(F32), axis=0),
            jnp.sum(grad_qkv_parts[2].astype(F32), axis=0),
        ]
    )
    grad_gain_a = jnp.sum(grad_one * normed_one, axis=0)
    grad_shift_a = jnp.sum(grad_one, axis=0)
    grad_inputs = grad_middle + norm_backward(grad_one, normed_one, inverse_one, gain_a)

    mine = (lax.iota(jnp.int32, parts) == t_index)[None, :, None]

    def placed(values):
        return jnp.where(mine, values.reshape(n_dp, 1, -1), 0.0).reshape(everyone, -1)

    packed_grads = jnp.concatenate(
        [
            v.reshape(everyone, vec)
            for v in (
                grad_gain_a,
                grad_shift_a,
                grad_out_shift,
                grad_gain_b,
                grad_shift_b,
                grad_down_shift,
            )
        ]
        + [
            placed(grad_qv_shift.reshape(2, local_heads, n_dp, -1).transpose(2, 0, 1, 3)),
            placed(grad_up_shift.reshape(bias_up.shape[0], n_dp, -1).transpose(1, 0, 2)),
        ],
        axis=1,
    )
    packed_grads = (
        jnp.pad(packed_grads, ((0, 0), (0, pad)))
        .reshape((chips, 2, parts) + tile)
        .transpose(2, 1, 0, 3, 4)
    )
    summed_first, sums = reduce_call(
        grad_first.reshape(chips, 2, -1, grad_first.shape[1]), packed_grads, chips, parts
    )
    sums = sums.reshape(-1)
    sum_gain_a, sum_shift_a, sum_out_shift, sum_gain_b, sum_shift_b, sum_down_shift = (
        sums[n * vec : (n + 1) * vec] for n in range(6)
    )
    summed_qkv = jnp.stack([summed_first[:, n * width : (n + 1) * width] for n in range(3)])
    return (
        output.astype(BF16),
        grad_inputs.astype(BF16),
        sum_gain_a,
        sum_shift_a,
        summed_qkv,
        sums[at : at + n_qv].reshape(bias_qv.shape),
        summed_first[:, 3 * width :].T,
        sum_out_shift,
        sum_gain_b,
        sum_shift_b,
        summed_up,
        sums[at + n_qv : end].reshape(bias_up.shape),
        summed_down.T,
        sum_down_shift,
    )


def solution(mesh):
    return jax.shard_map(
        local,
        mesh=mesh,
        in_specs=(
            P(("dp", "tensor"), None),
            P(("dp", "tensor")),
            P(("dp", "tensor")),
            P(None, "dp", "tensor"),
            P(None, "tensor", "dp"),
            P("tensor", "dp"),
            P(("dp", "tensor")),
            P(("dp", "tensor")),
            P(("dp", "tensor")),
            P("dp", "tensor"),
            P("tensor", "dp"),
            P("tensor", "dp"),
            P(("dp", "tensor")),
            P(("dp", "tensor"), None),
        ),
        out_specs=(
            P(("dp", "tensor"), None),
            P(("dp", "tensor"), None),
            P(("dp", "tensor")),
            P(("dp", "tensor")),
            P(None, "dp", "tensor"),
            P(None, "tensor", "dp"),
            P("tensor", "dp"),
            P(("dp", "tensor")),
            P(("dp", "tensor")),
            P(("dp", "tensor")),
            P("dp", "tensor"),
            P("tensor", "dp"),
            P("tensor", "dp"),
            P(("dp", "tensor")),
        ),
        check_vma=False,
    )
```

```python
import functools
import math

import jax
import jax.numpy as jnp
from jax import lax
from jax.experimental import pallas as pl
from jax.experimental.pallas import tpu as pltpu
from jax.sharding import PartitionSpec as P

H = 16
HD = 64
SEQ_LEN = 1024
PAIR = 2 * HD
QB = 256

EPSILON = 1e-05
MASKED = -1e30
F32 = jnp.float32
BF16 = jnp.bfloat16


def normalize(values):
    centred = values - jnp.mean(values, axis=-1, keepdims=True)
    inverse = lax.rsqrt(jnp.mean(centred * centred, axis=-1, keepdims=True) + EPSILON)
    return (centred * inverse, inverse)


def norm_backward(grad, normed, inverse, gain):
    scaled = grad * gain
    return inverse * (
        scaled
        - jnp.mean(scaled, axis=-1, keepdims=True)
        - normed * jnp.mean(scaled * normed, axis=-1, keepdims=True)
    )


def smooth_gate(values):
    return jax.nn.gelu(values, approximate=True)


def mm(a, b):
    return lax.dot_general(a, b, (((1,), (0,)), ((), ())), preferred_element_type=F32)


def mm_t(a, b):
    return lax.dot_general(a, b, (((1,), (1,)), ((), ())), preferred_element_type=F32)


def t_mm(a, b):
    return lax.dot_general(a, b, (((0,), (0,)), ((), ())), preferred_element_type=F32)


def head_masked(values, head):
    lane = lax.broadcasted_iota(jnp.int32, values.shape, 1)
    return jnp.where(lane // HD == head, values, jnp.zeros_like(values))


def stored_row(flip, position, length):
    half = length // 2
    return pl.multiple_of(((position // half + flip) % 2) * half + position % half, QB)


def attend_kernel(flip_ref, slope_ref, q_ref, k_ref, v_ref, o_ref, k_all, v_all):
    length = q_ref.shape[0]
    half = length // 2
    flip = flip_ref[0]
    first = pl.program_id(1) * 2
    for number in range(2):
        rows = pl.ds(stored_row(flip, number * half, length), half)
        k_all[number * half : (number + 1) * half] = k_ref[rows, :]
        v_all[number * half : (number + 1) * half] = v_ref[rows, :]
    for start in range(0, length, QB):
        end = start + QB
        q = q_ref[pl.ds(stored_row(flip, start, length), QB), :]
        q = (q.astype(F32) * (1.0 / math.sqrt(HD))).astype(BF16)
        offset = (
            lax.broadcasted_iota(jnp.int32, (1, end), 1) - start
        ).astype(F32)
        row = lax.broadcasted_iota(jnp.int32, (QB, QB), 0)
        col = lax.broadcasted_iota(jnp.int32, (QB, QB), 1)
        outs = []
        for head in range(2):
            scores = mm_t(head_masked(q, head), k_all[:end]) + slope_ref[first + head] * offset
            diagonal = jnp.where(col <= row, scores[:, start:], MASKED)
            scores = (
                jnp.concatenate([scores[:, :start], diagonal], axis=1) if start else diagonal
            )
            top = jnp.max(scores, axis=-1, keepdims=True)
            exponent = jnp.exp(scores - top)
            total = jnp.sum(exponent, axis=-1, keepdims=True)
            outs.append(mm(exponent.astype(BF16), v_all[:end]) / total)
        lane = lax.broadcasted_iota(jnp.int32, (QB, PAIR), 1)
        o_ref[pl.ds(stored_row(flip, start, length), QB), :] = jnp.where(
            lane < HD, outs[0], outs[1]
        ).astype(BF16)


def attend_back_kernel(
    flip_ref, slope_ref, q_ref, k_ref, v_ref, g_ref, dq_ref, dk_ref, dv_ref, k_all, v_all, dk, dv
):
    length = q_ref.shape[0]
    half = length // 2
    flip = flip_ref[0]
    first = pl.program_id(1) * 2
    for number in range(2):
        rows = pl.ds(stored_row(flip, number * half, length), half)
        k_all[number * half : (number + 1) * half] = k_ref[rows, :]
        v_all[number * half : (number + 1) * half] = v_ref[rows, :]
    for start in reversed(range(0, length, QB)):
        end = start + QB
        here = pl.ds(stored_row(flip, start, length), QB)
        q = (q_ref[here, :].astype(F32) * (1.0 / math.sqrt(HD))).astype(BF16)
        g = g_ref[here, :]
        offset = (lax.broadcasted_iota(jnp.int32, (end, 1), 0) - start).astype(F32)
        key = lax.broadcasted_iota(jnp.int32, (QB, QB), 0)
        query = lax.broadcasted_iota(jnp.int32, (QB, QB), 1)
        dq_sum = None
        dk_sum = None
        dv_sum = None
        for head in range(2):
            q_head = head_masked(q, head)
            g_head = head_masked(g, head)
            scores = mm_t(k_all[:end], q_head) + slope_ref[first + head] * offset
            diagonal = jnp.where(key <= query, scores[start:], MASKED)
            scores = (
                jnp.concatenate([scores[:start], diagonal], axis=0) if start else diagonal
            )
            top = jnp.max(scores, axis=0, keepdims=True)
            exponent = jnp.exp(scores - top)
            probs = exponent * (1.0 / jnp.sum(exponent, axis=0, keepdims=True))
            grad_probs = mm_t(v_all[:end], g_head)
            inner = jnp.sum(probs * grad_probs, axis=0, keepdims=True)
            grad_scores = (probs * (grad_probs - inner)).astype(BF16)
            dq_part = t_mm(grad_scores, head_masked(k_all[:end], head))
            dk_part = mm(grad_scores, q_head)
            dv_part = mm(probs.astype(BF16), g_head)
            dq_sum = dq_part if dq_sum is None else dq_sum + dq_part
            dk_sum = dk_part if dk_sum is None else dk_sum + dk_part
            dv_sum = dv_part if dv_sum is None else dv_sum + dv_part
        dq_ref[here, :] = (dq_sum * (1.0 / math.sqrt(HD))).astype(BF16)
        if end == length:
            dk[...] = dk_sum
            dv[...] = dv_sum
        else:
            dk[:end] += dk_sum
            dv[:end] += dv_sum
    for number in range(2):
        rows = pl.ds(stored_row(flip, number * half, length), half)
        dk_ref[rows, :] = dk[number * half : (number + 1) * half].astype(BF16)
        dv_ref[rows, :] = dv[number * half : (number + 1) * half].astype(BF16)


def attention_call(kernel, flip, slopes, operands, n_out, scratch, length, costs):
    group, width = operands[0].shape
    block = pl.BlockSpec((length, PAIR), lambda s, h: (s, h))
    scalar = pl.BlockSpec(memory_space=pltpu.SMEM)
    shape = jax.ShapeDtypeStruct((group, width), BF16)
    return pl.pallas_call(
        kernel,
        grid=(group // length, width // PAIR),
        out_shape=[shape] * n_out,
        in_specs=[scalar, scalar] + [block] * len(operands),
        out_specs=[block] * n_out,
        scratch_shapes=scratch,
        compiler_params=pltpu.CompilerParams(vmem_limit_bytes=48 * 1024 * 1024),
        cost_estimate=costs,
    )(flip, slopes, *operands)


def ring_place(chip, chips):
    return chip // 2 + (chip % 2) * (chips - 1 - 2 * (chip // 2))


def ring_chip(place, chips):
    place = lax.rem(place + 2 * chips, chips)
    far = place // (chips // 2)
    return far * (2 * (chips - 1 - place) + 1) + (1 - far) * 2 * place


def remote(src, dst, send, recv, device):
    return pltpu.make_async_remote_copy(
        src_ref=src,
        dst_ref=dst,
        send_sem=send,
        recv_sem=recv,
        device_id=device,
        device_id_type=pl.DeviceIdType.MESH,
    )


def greet(devices):
    barrier = pltpu.get_barrier_semaphore()
    for device in devices:
        pl.semaphore_signal(barrier, inc=1, device_id=device, device_id_type=pl.DeviceIdType.MESH)
    pl.semaphore_wait(barrier, len(devices))


def neighbours(chips, parts):
    index = lax.axis_index("dp")
    tensor = lax.axis_index("tensor")
    core = lax.rem(index, 2)
    place = ring_place(index // 2, chips)
    right = (ring_chip(place + 1, chips) * 2 + core, tensor)
    left = (ring_chip(place - 1, chips) * 2 + core, tensor)
    twin = (index + 1 - 2 * core, tensor)
    peers = [(index, lax.rem(tensor + k, parts)) for k in range(1, parts)]
    return core, place, tensor, right, left, twin, peers


def gather_kernel(chips, parts, *refs):
    pair = parts == 2
    if pair:
        x_ref, small_ref, tok_ref, cot_ref, full_ref, all_ref, other_ref, other_cot_ref = refs[:8]
        sems = refs[8:]
    else:
        x_ref, small_ref, full_ref, all_ref = refs[:4]
        sems = refs[4:]
    here_sem, big_s, big_r, swap_s, swap_r, sm_s, sm_r, smw_s, smw_r, ten_s, ten_r, tok_s, tok_r = sems
    core, place, tensor, right, left, twin, peers = neighbours(chips, parts)
    mine = ring_chip(place, chips)
    steps = chips // 2
    half = x_ref.shape[0] // 2
    greet([right, left, twin] + peers)
    waits = []
    if pair:
        tok = remote(tok_ref, other_ref, tok_s.at[0], tok_r.at[0], peers[0])
        tok.start()
    here = pltpu.make_async_copy(x_ref, full_ref.at[mine, core], here_sem.at[0])
    here.start()
    here_small = pltpu.make_async_copy(small_ref, all_ref.at[tensor, mine, core], here_sem.at[1])
    here_small.start()
    swaps = []
    small_swaps = []

    def swap(chip, first):
        n = len(swaps)
        small_src = small_ref if first else all_ref.at[tensor, chip, core]
        copy = remote(small_src, all_ref.at[tensor, chip, core], smw_s.at[n], smw_r.at[n], twin)
        copy.start()
        small_swaps.append(copy)
        src = x_ref if first else full_ref.at[chip, core]
        copy = remote(src, full_ref.at[chip, core], swap_s.at[n], swap_r.at[n], twin)
        copy.start()
        swaps.append(copy)

    previous = []
    for step in range(steps):
        started = []
        for copy in previous:
            copy.wait_recv()
        for side, device in ((0, right), (1, left)):
            chip = ring_chip(place - step if side == 0 else place + step, chips)
            slot = side * steps + step
            if step < steps - 1 or side == 0:
                src = small_ref if step == 0 else all_ref.at[tensor, chip, core]
                copy = remote(
                    src, all_ref.at[tensor, chip, core], sm_s.at[slot], sm_r.at[slot], device
                )
                copy.start()
                started.append(copy)
            src = x_ref if step == 0 else full_ref.at[chip, core]
            dst = full_ref.at[chip, core]
            if step == steps - 1:
                rows = pl.ds(side * half, half)
                src, dst = src.at[rows], dst.at[rows]
            copy = remote(src, dst, big_s.at[slot], big_r.at[slot], device)
            copy.start()
            started.append(copy)
        if pair and step == 1:
            cot = remote(cot_ref, other_cot_ref, tok_s.at[1], tok_r.at[1], peers[0])
            cot.start()
        if step == 0:
            swap(mine, True)
        else:
            swap(ring_chip(place - step, chips), False)
            swap(ring_chip(place + step, chips), False)
        waits += started
        previous = started
    for copy in previous:
        copy.wait_recv()
    swap(ring_chip(place + steps, chips), False)
    here_small.wait()
    for copy in small_swaps:
        copy.wait_recv()
    spread = []
    for k, peer in enumerate(peers):
        copy = remote(all_ref.at[tensor], all_ref.at[tensor], ten_s.at[k], ten_r.at[k], peer)
        copy.start()
        spread.append(copy)
    here.wait()
    for copy in swaps:
        copy.wait_recv()
    for copy in waits + swaps + small_swaps:
        copy.wait_send()
    for copy in spread:
        copy.wait()
    if pair:
        tok.wait()
        cot.wait()


def gather_call(shard, small, tokens, cotangent, chips, parts):
    rows, columns = shard.shape
    anywhere = pl.BlockSpec(memory_space=pl.ANY)
    out = [
        jax.ShapeDtypeStruct((chips, 2, rows, columns), BF16),
        jax.ShapeDtypeStruct((parts, chips, 2) + small.shape, F32),
    ]
    operands = [shard, small]
    if parts == 2:
        out += [jax.ShapeDtypeStruct(tokens.shape, BF16)] * 2
        operands += [tokens, cotangent]
    sem = pltpu.SemaphoreType.DMA
    result = pl.pallas_call(
        functools.partial(gather_kernel, chips, parts),
        out_shape=out,
        in_specs=[anywhere] * len(operands),
        out_specs=[anywhere] * len(out),
        scratch_shapes=[sem((2,))]
        + [sem((chips,))] * 8
        + [sem((parts - 1,))] * 2
        + [sem((2,))] * 2,
        compiler_params=pltpu.CompilerParams(collective_id=0, has_side_effects=True),
        cost_estimate=pl.CostEstimate(
            flops=0, bytes_accessed=64 * rows * columns, transcendentals=0
        ),
    )(*operands)
    return list(result) + [None] * (4 - len(out))


def reduce_kernel(chips, parts, g_ref, s_ref, o_ref, so_ref, *scratch):
    (pair_in, ring_in, ring_out, sm_ten, sm_sum, sm_pair, sm_in, sm_out) = scratch[:8]
    pair_s, pair_r, big_s, big_r, ten_s, ten_r, smp_s, smp_r, sm_s, sm_r = scratch[8:]
    core, place, tensor, right, left, twin, peers = neighbours(chips, parts)
    steps = chips // 2
    half = g_ref.shape[2] // 2
    greet([right, left, twin] + peers)
    order = [steps]
    for n in reversed(range(1, steps)):
        order += [-n, n]
    order.append(0)
    away = 1 - core
    done = []
    ten = []
    for k, peer in enumerate(peers):
        goal = lax.rem(tensor + k + 1, parts)
        copy = remote(s_ref.at[goal], sm_ten.at[k], ten_s.at[k], ten_r.at[k], peer)
        copy.start()
        ten.append(copy)
    pairs = {}
    for n, shift in enumerate(order):
        chip = ring_chip(place + shift, chips)
        copy = remote(g_ref.at[chip, away], pair_in.at[n], pair_s.at[n], pair_r.at[n], twin)
        copy.start()
        pairs[shift] = (n, copy)

    def own(shift):
        n, copy = pairs[shift]
        if shift not in done:
            copy.wait_recv()
            done.append(shift)
        chip = ring_chip(place + shift, chips)
        return g_ref[chip, core].astype(F32) + pair_in[n].astype(F32)

    sends = list(ten)
    arrived = {}
    small_arrived = {}

    def own_small(shift):
        chip = ring_chip(place + shift, chips)
        return sm_sum[core, chip] + sm_pair[chip]

    def small_step(step):
        for side, device in ((0, left), (1, right)):
            if step == 0 and side == 1:
                continue
            shift = (step - steps) if side == 0 else (steps - step)
            slot = side * steps + step
            value = own_small(shift)
            if side in small_arrived:
                small_arrived[side].wait_recv()
                value = value + sm_in[slot - 1]
            sm_out[slot] = value
            copy = remote(sm_out.at[slot], sm_in.at[slot], sm_s.at[slot], sm_r.at[slot], device)
            copy.start()
            small_arrived[side] = copy
            sends.append(copy)

    for step in range(steps):
        for side, device in ((0, left), (1, right)):
            shift = (step - steps) if side == 0 else (steps - step)
            slot = side * steps + step
            if step == 0:
                rows = pl.ds(side * half, half)
                ring_out[slot] = own(steps).astype(BF16)
                copy = remote(
                    ring_out.at[slot, rows],
                    ring_in.at[slot, rows],
                    big_s.at[slot],
                    big_r.at[slot],
                    device,
                )
            else:
                value = own(shift)
                arrived[side].wait_recv()
                if step == 1:
                    rows = slice(side * half, (side + 1) * half)
                    rest = slice((1 - side) * half, (2 - side) * half)
                    ring_out[slot, rows] = (
                        value[rows] + ring_in[slot - 1, rows].astype(F32)
                    ).astype(BF16)
                    ring_out[slot, rest] = value[rest].astype(BF16)
                else:
                    ring_out[slot] = (value + ring_in[slot - 1].astype(F32)).astype(BF16)
                copy = remote(
                    ring_out.at[slot], ring_in.at[slot], big_s.at[slot], big_r.at[slot], device
                )
            copy.start()
            arrived[side] = copy
            sends.append(copy)
        if step == 0:
            for copy in ten:
                copy.wait_recv()
            total = s_ref[tensor]
            for k in range(len(peers)):
                total = total + sm_ten[k]
            sm_sum[...] = total
            sm_pair_copy = remote(sm_sum.at[away], sm_pair, smp_s.at[0], smp_r.at[0], twin)
            sm_pair_copy.start()
        elif step == 1:
            sm_pair_copy.wait_recv()
            small_step(0)
        else:
            small_step(step - 1)
    small_step(steps - 1)
    value = own(0)
    for side in range(2):
        arrived[side].wait_recv()
        value = value + ring_in[(side + 1) * steps - 1].astype(F32)
    o_ref[...] = value
    value = own_small(0)
    for side in range(2):
        small_arrived[side].wait_recv()
        value = value + sm_in[(side + 1) * steps - 1]
    so_ref[...] = value
    for _, copy in pairs.values():
        copy.wait_send()
    sm_pair_copy.wait_send()
    for copy in sends:
        copy.wait_send()


def reduce_call(grad, small, chips, parts):
    rows, columns = grad.shape[2:]
    tile = small.shape[3:]
    sem = pltpu.SemaphoreType.DMA
    vmem = pl.BlockSpec(memory_space=pltpu.VMEM)
    return pl.pallas_call(
        functools.partial(reduce_kernel, chips, parts),
        out_shape=[
            jax.ShapeDtypeStruct((rows, columns), F32),
            jax.ShapeDtypeStruct(tile, F32),
        ],
        in_specs=[vmem, vmem],
        out_specs=[vmem, vmem],
        scratch_shapes=[
            pltpu.VMEM((chips, rows, columns), BF16),
            pltpu.VMEM((chips, rows, columns), BF16),
            pltpu.VMEM((chips, rows, columns), BF16),
            pltpu.VMEM((parts - 1, 2, chips) + tile, F32),
            pltpu.VMEM((2, chips) + tile, F32),
            pltpu.VMEM((chips,) + tile, F32),
            pltpu.VMEM((chips,) + tile, F32),
            pltpu.VMEM((chips,) + tile, F32),
        ]
        + [sem((chips,))] * 4
        + [sem((parts - 1,))] * 2
        + [sem((1,))] * 2
        + [sem((chips,))] * 2,
        compiler_params=pltpu.CompilerParams(
            collective_id=1, has_side_effects=True, vmem_limit_bytes=40 * 1024 * 1024
        ),
        cost_estimate=pl.CostEstimate(
            flops=0, bytes_accessed=64 * rows * columns, transcendentals=0
        ),
    )(grad, small)


def local(
    tokens,
    gain_one,
    shift_one,
    w_qkv,
    bias_qv,
    w_out,
    bias_out,
    gain_two,
    shift_two,
    w_up,
    bias_up,
    w_down,
    bias_down,
    cotangent,
):
    parts = lax.axis_size("tensor")
    n_dp = lax.axis_size("dp")
    everyone = n_dp * parts
    t_index = lax.axis_index("tensor")
    chips = n_dp // 2

    def gather_weight(shard):
        return lax.all_gather(shard, "dp", axis=0, tiled=True)

    def scatter_weight(grad):
        return lax.psum_scatter(grad, "dp", scatter_dimension=0, tiled=True).astype(F32)

    def gather_rows(mine):
        if parts == 2:
            return [mine, lax.ppermute(mine, "tensor", [(0, 1), (1, 0)])]
        return [lax.all_gather(mine, "tensor", axis=0, tiled=True)]

    def scatter_rows(product, blocks):
        if parts == 2:
            sent = lax.ppermute(product(blocks[1]).astype(BF16), "tensor", [(0, 1), (1, 0)])
            return product(blocks[0]) + sent.astype(F32)
        return lax.psum_scatter(
            product(blocks[0]).astype(BF16), "tensor", scatter_dimension=0, tiled=True
        ).astype(F32)

    def joined(blocks):
        return blocks[0] if len(blocks) == 1 else jnp.concatenate(blocks, axis=0)

    def split(rows):
        if parts == 2:
            return [rows[: rows.shape[0] // 2], rows[rows.shape[0] // 2 :]]
        return [rows]

    vec = gain_one.shape[0]
    n_qv = bias_qv.size
    n_bu = bias_up.size
    packed = jnp.concatenate(
        [gain_one, shift_one, bias_out, gain_two, shift_two, bias_down]
        + [bias_qv.astype(F32).reshape(-1), bias_up.astype(F32).reshape(-1)]
    )
    tile = (8, 128)
    pad = tile[0] * tile[1] - packed.size
    first_shard = jnp.concatenate([w_qkv[0], w_qkv[1], w_qkv[2], w_out.T], axis=1)
    first_full, small, other_tokens, other_cot = gather_call(
        first_shard, jnp.pad(packed, (0, pad)).reshape(tile), tokens, cotangent, chips, parts
    )
    first_full = first_full.reshape(-1, first_shard.shape[1])
    small = small.reshape(parts, n_dp, -1).transpose(1, 0, 2).reshape(everyone, -1)
    gain_a, shift_a, out_shift, gain_b, shift_b, down_shift = (
        small[:, n * vec : (n + 1) * vec].reshape(-1) for n in range(6)
    )
    at = 6 * vec
    end = at + n_qv + n_bu
    local_small = lax.dynamic_index_in_dim(
        small.reshape(n_dp, parts, -1), t_index, 1, keepdims=False
    )
    local_heads = bias_qv.shape[1]
    width = local_heads * HD
    qv_shift = (
        local_small[:, at : at + n_qv]
        .reshape(n_dp, 2, local_heads, -1)
        .transpose(1, 2, 0, 3)
        .reshape(2, width)
    )
    up_shift = (
        local_small[:, at + n_qv : end]
        .reshape(n_dp, bias_up.shape[0], -1)
        .transpose(1, 0, 2)
        .reshape(-1)
    )
    hidden_units = up_shift.shape[0]

    up_full = gather_weight(w_up)
    down_t = gather_weight(w_down.T)
    qkv_full = first_full[:, : 3 * width]
    out_t = first_full[:, 3 * width :]

    rows = tokens.shape[0]
    group = rows * parts
    length = min(SEQ_LEN, group)
    sequences = group // length
    head_ids = t_index * local_heads + lax.iota(jnp.int32, local_heads)
    slopes = jnp.exp2(-8.0 * (head_ids + 1).astype(F32) / H)
    flip = (t_index if parts == 2 else 0 * t_index).astype(jnp.int32).reshape(1)

    cot_blocks = [cotangent, other_cot] if parts == 2 else gather_rows(cotangent)
    inputs = tokens.astype(F32)
    normed_one, inverse_one = normalize(inputs)
    low_one = (normed_one * gain_a + shift_a).astype(BF16)
    if parts == 2:
        other_normed = normalize(other_tokens.astype(F32))[0]
        one_blocks = [low_one, (other_normed * gain_a + shift_a).astype(BF16)]
    else:
        one_blocks = gather_rows(low_one)
    qkv_shift = jnp.concatenate([qv_shift[0], jnp.zeros((width,), F32), qv_shift[1]])
    qkv_low = joined([(mm(b, qkv_full) + qkv_shift).astype(BF16) for b in one_blocks])
    query, keys, values = (qkv_low[:, n * width : (n + 1) * width] for n in range(3))
    pair_area = sequences * local_heads * length * length
    vmem = pltpu.VMEM((length, PAIR), BF16)
    (attended,) = attention_call(
        attend_kernel,
        flip,
        slopes,
        (query, keys, values),
        1,
        [vmem, vmem],
        length,
        pl.CostEstimate(
            flops=4 * PAIR * pair_area, bytes_accessed=8 * group * width, transcendentals=pair_area
        ),
    )
    middle = (
        inputs + scatter_rows(lambda b: mm_t(b, out_t), split(attended)) + out_shift
    )
    normed_two, inverse_two = normalize(middle)
    two_blocks = gather_rows((normed_two * gain_b + shift_b).astype(BF16))
    hidden = [mm(b, up_full) + up_shift for b in two_blocks]
    gated = [smooth_gate(h).astype(BF16) for h in hidden]
    grad_gated = [mm(c, down_t) for c in cot_blocks]
    grad_hidden = [
        jax.vjp(smooth_gate, h)[1](g)[0].astype(BF16) for h, g in zip(hidden, grad_gated)
    ]
    grad_two = scatter_rows(lambda b: mm_t(b, up_full), grad_hidden)

    cot_all = joined(cot_blocks)
    grad_hidden_all = joined(grad_hidden)
    summed_down = scatter_weight(t_mm(cot_all, joined(gated)).astype(BF16))
    summed_up = scatter_weight(t_mm(joined(two_blocks), grad_hidden_all).astype(BF16))
    grad_up_shift = jnp.sum(grad_hidden_all.astype(F32), axis=0)

    grad_out_rows = cotangent.astype(F32)
    grad_down_shift = jnp.sum(grad_out_rows, axis=0)
    grad_gain_b = jnp.sum(grad_two * normed_two, axis=0)
    grad_shift_b = jnp.sum(grad_two, axis=0)
    grad_middle = grad_out_rows + norm_backward(grad_two, normed_two, inverse_two, gain_b)
    grad_out_shift = jnp.sum(grad_middle, axis=0)
    low_blocks = gather_rows(grad_middle.astype(BF16))
    grad_attended = joined([mm(b, out_t).astype(BF16) for b in low_blocks])
    if parts == 2:
        late = lax.optimization_barrier((*gated, low_blocks[1]))[:2]
        away = mm_t(late[1], down_t).astype(BF16)
        grad_attended, away = lax.optimization_barrier((grad_attended, away))
        came = lax.ppermute(away, "tensor", [(0, 1), (1, 0)])
        feed = mm_t(late[0], down_t) + came.astype(F32)
    else:
        feed = scatter_rows(lambda b: mm_t(b, down_t), gated)
    output = middle + feed + down_shift
    scratch = [vmem, vmem] + [pltpu.VMEM((length, PAIR), F32)] * 2
    grad_qkv_parts = attention_call(
        attend_back_kernel,
        flip,
        slopes,
        (query, keys, values, grad_attended),
        3,
        scratch,
        length,
        pl.CostEstimate(
            flops=10 * PAIR * pair_area,
            bytes_accessed=14 * group * width,
            transcendentals=pair_area,
        ),
    )
    grad_qkv_rows = jnp.concatenate(grad_qkv_parts, axis=1)
    grad_one = scatter_rows(lambda b: mm_t(b, qkv_full), split(grad_qkv_rows))
    grad_first = jnp.concatenate(
        [
            t_mm(joined(one_blocks), grad_qkv_rows).astype(BF16),
            t_mm(joined(low_blocks), attended).astype(BF16),
        ],
        axis=1,
    )
    grad_qv_shift = jnp.stack(
        [
            jnp.sum(grad_qkv_parts[0].astype(F32), axis=0),
            jnp.sum(grad_qkv_parts[2].astype(F32), axis=0),
        ]
    )
    grad_gain_a = jnp.sum(grad_one * normed_one, axis=0)
    grad_shift_a = jnp.sum(grad_one, axis=0)
    grad_inputs = grad_middle + norm_backward(grad_one, normed_one, inverse_one, gain_a)

    mine = (lax.iota(jnp.int32, parts) == t_index)[None, :, None]

    def placed(values):
        return jnp.where(mine, values.reshape(n_dp, 1, -1), 0.0).reshape(everyone, -1)

    packed_grads = jnp.concatenate(
        [
            v.reshape(everyone, vec)
            for v in (
                grad_gain_a,
                grad_shift_a,
                grad_out_shift,
                grad_gain_b,
                grad_shift_b,
                grad_down_shift,
            )
        ]
        + [
            placed(grad_qv_shift.reshape(2, local_heads, n_dp, -1).transpose(2, 0, 1, 3)),
            placed(grad_up_shift.reshape(bias_up.shape[0], n_dp, -1).transpose(1, 0, 2)),
        ],
        axis=1,
    )
    packed_grads = (
        jnp.pad(packed_grads, ((0, 0), (0, pad)))
        .reshape((chips, 2, parts) + tile)
        .transpose(2, 1, 0, 3, 4)
    )
    summed_first, sums = reduce_call(
        grad_first.reshape(chips, 2, -1, grad_first.shape[1]), packed_grads, chips, parts
    )
    sums = sums.reshape(-1)
    sum_gain_a, sum_shift_a, sum_out_shift, sum_gain_b, sum_shift_b, sum_down_shift = (
        sums[n * vec : (n + 1) * vec] for n in range(6)
    )
    summed_qkv = jnp.stack([summed_first[:, n * width : (n + 1) * width] for n in range(3)])
    return (
        output.astype(BF16),
        grad_inputs.astype(BF16),
        sum_gain_a,
        sum_shift_a,
        summed_qkv,
        sums[at : at + n_qv].reshape(bias_qv.shape),
        summed_first[:, 3 * width :].T,
        sum_out_shift,
        sum_gain_b,
        sum_shift_b,
        summed_up,
        sums[at + n_qv : end].reshape(bias_up.shape),
        summed_down.T,
        sum_down_shift,
    )


def solution(mesh):
    return jax.shard_map(
        local,
        mesh=mesh,
        in_specs=(
            P(("dp", "tensor"), None),
            P(("dp", "tensor")),
            P(("dp", "tensor")),
            P(None, "dp", "tensor"),
            P(None, "tensor", "dp"),
            P("tensor", "dp"),
            P(("dp", "tensor")),
            P(("dp", "tensor")),
            P(("dp", "tensor")),
            P("dp", "tensor"),
            P("tensor", "dp"),
            P("tensor", "dp"),
            P(("dp", "tensor")),
            P(("dp", "tensor"), None),
        ),
        out_specs=(
            P(("dp", "tensor"), None),
            P(("dp", "tensor"), None),
            P(("dp", "tensor")),
            P(("dp", "tensor")),
            P(None, "dp", "tensor"),
            P(None, "tensor", "dp"),
            P("tensor", "dp"),
            P(("dp", "tensor")),
            P(("dp", "tensor")),
            P(("dp", "tensor")),
            P("dp", "tensor"),
            P("tensor", "dp"),
            P("tensor", "dp"),
            P(("dp", "tensor")),
        ),
        check_vma=False,
    )
```

```python
import functools
import math

import jax
import jax.numpy as jnp
from jax import lax
from jax.experimental import pallas as pl
from jax.experimental.pallas import tpu as pltpu
from jax.sharding import PartitionSpec as P

H = 16
HD = 64
SEQ_LEN = 1024
PAIR = 2 * HD
QB = 256

EPSILON = 1e-05
MASKED = -1e30
F32 = jnp.float32
BF16 = jnp.bfloat16


def normalize(values):
    centred = values - jnp.mean(values, axis=-1, keepdims=True)
    inverse = lax.rsqrt(jnp.mean(centred * centred, axis=-1, keepdims=True) + EPSILON)
    return (centred * inverse, inverse)


def norm_backward(grad, normed, inverse, gain):
    scaled = grad * gain
    return inverse * (
        scaled
        - jnp.mean(scaled, axis=-1, keepdims=True)
        - normed * jnp.mean(scaled * normed, axis=-1, keepdims=True)
    )


def smooth_gate(values):
    return jax.nn.gelu(values, approximate=True)


def mm(a, b):
    return lax.dot_general(a, b, (((1,), (0,)), ((), ())), preferred_element_type=F32)


def mm_t(a, b):
    return lax.dot_general(a, b, (((1,), (1,)), ((), ())), preferred_element_type=F32)


def t_mm(a, b):
    return lax.dot_general(a, b, (((0,), (0,)), ((), ())), preferred_element_type=F32)


def head_masked(values, head):
    lane = lax.broadcasted_iota(jnp.int32, values.shape, 1)
    return jnp.where(lane // HD == head, values, jnp.zeros_like(values))


def stored_row(flip, position, length):
    half = length // 2
    return pl.multiple_of(((position // half + flip) % 2) * half + position % half, QB)


def attend_kernel(flip_ref, slope_ref, q_ref, k_ref, v_ref, o_ref, k_all, v_all):
    length = q_ref.shape[0]
    half = length // 2
    flip = flip_ref[0]
    first = pl.program_id(1) * 2
    for number in range(2):
        rows = pl.ds(stored_row(flip, number * half, length), half)
        k_all[number * half : (number + 1) * half] = k_ref[rows, :]
        v_all[number * half : (number + 1) * half] = v_ref[rows, :]
    for start in range(0, length, QB):
        end = start + QB
        q = q_ref[pl.ds(stored_row(flip, start, length), QB), :]
        q = (q.astype(F32) * (1.0 / math.sqrt(HD))).astype(BF16)
        offset = (
            lax.broadcasted_iota(jnp.int32, (1, end), 1) - start
        ).astype(F32)
        row = lax.broadcasted_iota(jnp.int32, (QB, QB), 0)
        col = lax.broadcasted_iota(jnp.int32, (QB, QB), 1)
        outs = []
        for head in range(2):
            scores = mm_t(head_masked(q, head), k_all[:end]) + slope_ref[first + head] * offset
            diagonal = jnp.where(col <= row, scores[:, start:], MASKED)
            scores = (
                jnp.concatenate([scores[:, :start], diagonal], axis=1) if start else diagonal
            )
            top = jnp.max(scores, axis=-1, keepdims=True)
            exponent = jnp.exp(scores - top)
            total = jnp.sum(exponent, axis=-1, keepdims=True)
            outs.append(mm(exponent.astype(BF16), v_all[:end]) / total)
        lane = lax.broadcasted_iota(jnp.int32, (QB, PAIR), 1)
        o_ref[pl.ds(stored_row(flip, start, length), QB), :] = jnp.where(
            lane < HD, outs[0], outs[1]
        ).astype(BF16)


def attend_back_kernel(
    flip_ref, slope_ref, q_ref, k_ref, v_ref, g_ref, dq_ref, dk_ref, dv_ref, k_all, v_all, dk, dv
):
    length = q_ref.shape[0]
    half = length // 2
    flip = flip_ref[0]
    first = pl.program_id(1) * 2
    for number in range(2):
        rows = pl.ds(stored_row(flip, number * half, length), half)
        k_all[number * half : (number + 1) * half] = k_ref[rows, :]
        v_all[number * half : (number + 1) * half] = v_ref[rows, :]
    for start in reversed(range(0, length, QB)):
        end = start + QB
        here = pl.ds(stored_row(flip, start, length), QB)
        q = (q_ref[here, :].astype(F32) * (1.0 / math.sqrt(HD))).astype(BF16)
        g = g_ref[here, :]
        offset = (lax.broadcasted_iota(jnp.int32, (end, 1), 0) - start).astype(F32)
        key = lax.broadcasted_iota(jnp.int32, (QB, QB), 0)
        query = lax.broadcasted_iota(jnp.int32, (QB, QB), 1)
        dq_sum = None
        dk_sum = None
        dv_sum = None
        for head in range(2):
            q_head = head_masked(q, head)
            g_head = head_masked(g, head)
            scores = mm_t(k_all[:end], q_head) + slope_ref[first + head] * offset
            diagonal = jnp.where(key <= query, scores[start:], MASKED)
            scores = (
                jnp.concatenate([scores[:start], diagonal], axis=0) if start else diagonal
            )
            top = jnp.max(scores, axis=0, keepdims=True)
            exponent = jnp.exp(scores - top)
            probs = exponent * (1.0 / jnp.sum(exponent, axis=0, keepdims=True))
            grad_probs = mm_t(v_all[:end], g_head)
            inner = jnp.sum(probs * grad_probs, axis=0, keepdims=True)
            grad_scores = (probs * (grad_probs - inner)).astype(BF16)
            dq_part = t_mm(grad_scores, head_masked(k_all[:end], head))
            dk_part = mm(grad_scores, q_head)
            dv_part = mm(probs.astype(BF16), g_head)
            dq_sum = dq_part if dq_sum is None else dq_sum + dq_part
            dk_sum = dk_part if dk_sum is None else dk_sum + dk_part
            dv_sum = dv_part if dv_sum is None else dv_sum + dv_part
        dq_ref[here, :] = (dq_sum * (1.0 / math.sqrt(HD))).astype(BF16)
        if end == length:
            dk[...] = dk_sum
            dv[...] = dv_sum
        else:
            dk[:end] += dk_sum
            dv[:end] += dv_sum
    for number in range(2):
        rows = pl.ds(stored_row(flip, number * half, length), half)
        dk_ref[rows, :] = dk[number * half : (number + 1) * half].astype(BF16)
        dv_ref[rows, :] = dv[number * half : (number + 1) * half].astype(BF16)


def attention_call(kernel, flip, slopes, operands, n_out, scratch, length, costs):
    group, width = operands[0].shape
    block = pl.BlockSpec((length, PAIR), lambda s, h: (s, h))
    scalar = pl.BlockSpec(memory_space=pltpu.SMEM)
    shape = jax.ShapeDtypeStruct((group, width), BF16)
    return pl.pallas_call(
        kernel,
        grid=(group // length, width // PAIR),
        out_shape=[shape] * n_out,
        in_specs=[scalar, scalar] + [block] * len(operands),
        out_specs=[block] * n_out,
        scratch_shapes=scratch,
        compiler_params=pltpu.CompilerParams(vmem_limit_bytes=48 * 1024 * 1024),
        cost_estimate=costs,
    )(flip, slopes, *operands)


def ring_place(chip, chips):
    return chip // 2 + (chip % 2) * (chips - 1 - 2 * (chip // 2))


def ring_chip(place, chips):
    place = lax.rem(place + 2 * chips, chips)
    far = place // (chips // 2)
    return far * (2 * (chips - 1 - place) + 1) + (1 - far) * 2 * place


def remote(src, dst, send, recv, device):
    return pltpu.make_async_remote_copy(
        src_ref=src,
        dst_ref=dst,
        send_sem=send,
        recv_sem=recv,
        device_id=device,
        device_id_type=pl.DeviceIdType.MESH,
    )


def greet(devices):
    barrier = pltpu.get_barrier_semaphore()
    for device in devices:
        pl.semaphore_signal(barrier, inc=1, device_id=device, device_id_type=pl.DeviceIdType.MESH)
    pl.semaphore_wait(barrier, len(devices))


def neighbours(chips, parts):
    index = lax.axis_index("dp")
    tensor = lax.axis_index("tensor")
    core = lax.rem(index, 2)
    place = ring_place(index // 2, chips)
    right = (ring_chip(place + 1, chips) * 2 + core, tensor)
    left = (ring_chip(place - 1, chips) * 2 + core, tensor)
    twin = (index + 1 - 2 * core, tensor)
    peers = [(index, lax.rem(tensor + k, parts)) for k in range(1, parts)]
    return core, place, tensor, right, left, twin, peers


def gather_kernel(chips, parts, *refs):
    pair = parts == 2
    if pair:
        x_ref, small_ref, tok_ref, cot_ref, full_ref, all_ref, other_ref, other_cot_ref = refs[:8]
        sems = refs[8:]
    else:
        x_ref, small_ref, full_ref, all_ref = refs[:4]
        sems = refs[4:]
    here_sem, big_s, big_r, swap_s, swap_r, sm_s, sm_r, smw_s, smw_r, ten_s, ten_r, tok_s, tok_r = sems
    core, place, tensor, right, left, twin, peers = neighbours(chips, parts)
    mine = ring_chip(place, chips)
    steps = chips // 2
    half = x_ref.shape[0] // 2
    greet([right, left, twin] + peers)
    waits = []
    if pair:
        tok = remote(tok_ref, other_ref, tok_s.at[0], tok_r.at[0], peers[0])
        tok.start()
    here = pltpu.make_async_copy(x_ref, full_ref.at[mine, core], here_sem.at[0])
    here.start()
    here_small = pltpu.make_async_copy(small_ref, all_ref.at[tensor, mine, core], here_sem.at[1])
    here_small.start()
    swaps = []
    small_swaps = []

    def swap(chip, first):
        n = len(swaps)
        small_src = small_ref if first else all_ref.at[tensor, chip, core]
        copy = remote(small_src, all_ref.at[tensor, chip, core], smw_s.at[n], smw_r.at[n], twin)
        copy.start()
        small_swaps.append(copy)
        src = x_ref if first else full_ref.at[chip, core]
        copy = remote(src, full_ref.at[chip, core], swap_s.at[n], swap_r.at[n], twin)
        copy.start()
        swaps.append(copy)

    previous = []
    for step in range(steps):
        started = []
        for copy in previous:
            copy.wait_recv()
        for side, device in ((0, right), (1, left)):
            chip = ring_chip(place - step if side == 0 else place + step, chips)
            slot = side * steps + step
            if step < steps - 1 or side == 0:
                src = small_ref if step == 0 else all_ref.at[tensor, chip, core]
                copy = remote(
                    src, all_ref.at[tensor, chip, core], sm_s.at[slot], sm_r.at[slot], device
                )
                copy.start()
                started.append(copy)
            src = x_ref if step == 0 else full_ref.at[chip, core]
            dst = full_ref.at[chip, core]
            if step == steps - 1:
                rows = pl.ds(side * half, half)
                src, dst = src.at[rows], dst.at[rows]
            copy = remote(src, dst, big_s.at[slot], big_r.at[slot], device)
            copy.start()
            started.append(copy)
        if pair and step == 1:
            cot = remote(cot_ref, other_cot_ref, tok_s.at[1], tok_r.at[1], peers[0])
            cot.start()
        if step == 0:
            swap(mine, True)
        else:
            swap(ring_chip(place - step, chips), False)
            swap(ring_chip(place + step, chips), False)
        waits += started
        previous = started
    for copy in previous:
        copy.wait_recv()
    swap(ring_chip(place + steps, chips), False)
    here_small.wait()
    for copy in small_swaps:
        copy.wait_recv()
    spread = []
    for k, peer in enumerate(peers):
        copy = remote(all_ref.at[tensor], all_ref.at[tensor], ten_s.at[k], ten_r.at[k], peer)
        copy.start()
        spread.append(copy)
    here.wait()
    for copy in swaps:
        copy.wait_recv()
    for copy in waits + swaps + small_swaps:
        copy.wait_send()
    for copy in spread:
        copy.wait()
    if pair:
        tok.wait()
        cot.wait()


def gather_call(shard, small, tokens, cotangent, chips, parts):
    rows, columns = shard.shape
    anywhere = pl.BlockSpec(memory_space=pl.ANY)
    out = [
        jax.ShapeDtypeStruct((chips, 2, rows, columns), BF16),
        jax.ShapeDtypeStruct((parts, chips, 2) + small.shape, F32),
    ]
    operands = [shard, small]
    if parts == 2:
        out += [jax.ShapeDtypeStruct(tokens.shape, BF16)] * 2
        operands += [tokens, cotangent]
    sem = pltpu.SemaphoreType.DMA
    result = pl.pallas_call(
        functools.partial(gather_kernel, chips, parts),
        out_shape=out,
        in_specs=[anywhere] * len(operands),
        out_specs=[anywhere] * len(out),
        scratch_shapes=[sem((2,))]
        + [sem((chips,))] * 8
        + [sem((parts - 1,))] * 2
        + [sem((2,))] * 2,
        compiler_params=pltpu.CompilerParams(collective_id=0, has_side_effects=True),
        cost_estimate=pl.CostEstimate(
            flops=0, bytes_accessed=64 * rows * columns, transcendentals=0
        ),
    )(*operands)
    return list(result) + [None] * (4 - len(out))


def reduce_kernel(chips, parts, g_ref, s_ref, o_ref, so_ref, *scratch):
    (pair_in, ring_in, ring_out, sm_ten, sm_sum, sm_pair, sm_in, sm_out) = scratch[:8]
    pair_s, pair_r, big_s, big_r, ten_s, ten_r, smp_s, smp_r, sm_s, sm_r = scratch[8:]
    core, place, tensor, right, left, twin, peers = neighbours(chips, parts)
    steps = chips // 2
    half = g_ref.shape[2] // 2
    greet([right, left, twin] + peers)
    order = [steps]
    for n in reversed(range(1, steps)):
        order += [-n, n]
    order.append(0)
    away = 1 - core
    done = []
    ten = []
    for k, peer in enumerate(peers):
        goal = lax.rem(tensor + k + 1, parts)
        copy = remote(s_ref.at[goal], sm_ten.at[k], ten_s.at[k], ten_r.at[k], peer)
        copy.start()
        ten.append(copy)
    pairs = {}
    for n, shift in enumerate(order):
        chip = ring_chip(place + shift, chips)
        copy = remote(g_ref.at[chip, away], pair_in.at[n], pair_s.at[n], pair_r.at[n], twin)
        copy.start()
        pairs[shift] = (n, copy)

    def own(shift):
        n, copy = pairs[shift]
        if shift not in done:
            copy.wait_recv()
            done.append(shift)
        chip = ring_chip(place + shift, chips)
        return g_ref[chip, core].astype(F32) + pair_in[n].astype(F32)

    sends = list(ten)
    arrived = {}
    small_arrived = {}

    def own_small(shift):
        chip = ring_chip(place + shift, chips)
        return sm_sum[core, chip] + sm_pair[chip]

    def small_step(step):
        for side, device in ((0, left), (1, right)):
            if step == 0 and side == 1:
                continue
            shift = (step - steps) if side == 0 else (steps - step)
            slot = side * steps + step
            value = own_small(shift)
            if side in small_arrived:
                small_arrived[side].wait_recv()
                value = value + sm_in[slot - 1]
            sm_out[slot] = value
            copy = remote(sm_out.at[slot], sm_in.at[slot], sm_s.at[slot], sm_r.at[slot], device)
            copy.start()
            small_arrived[side] = copy
            sends.append(copy)

    for step in range(steps):
        for side, device in ((0, left), (1, right)):
            shift = (step - steps) if side == 0 else (steps - step)
            slot = side * steps + step
            if step == 0:
                rows = pl.ds(side * half, half)
                ring_out[slot] = own(steps).astype(BF16)
                copy = remote(
                    ring_out.at[slot, rows],
                    ring_in.at[slot, rows],
                    big_s.at[slot],
                    big_r.at[slot],
                    device,
                )
            else:
                value = own(shift)
                arrived[side].wait_recv()
                if step == 1:
                    rows = slice(side * half, (side + 1) * half)
                    rest = slice((1 - side) * half, (2 - side) * half)
                    ring_out[slot, rows] = (
                        value[rows] + ring_in[slot - 1, rows].astype(F32)
                    ).astype(BF16)
                    ring_out[slot, rest] = value[rest].astype(BF16)
                else:
                    ring_out[slot] = (value + ring_in[slot - 1].astype(F32)).astype(BF16)
                copy = remote(
                    ring_out.at[slot], ring_in.at[slot], big_s.at[slot], big_r.at[slot], device
                )
            copy.start()
            arrived[side] = copy
            sends.append(copy)
        if step == 0:
            for copy in ten:
                copy.wait_recv()
            total = s_ref[tensor]
            for k in range(len(peers)):
                total = total + sm_ten[k]
            sm_sum[...] = total
            sm_pair_copy = remote(sm_sum.at[away], sm_pair, smp_s.at[0], smp_r.at[0], twin)
            sm_pair_copy.start()
        elif step == 1:
            sm_pair_copy.wait_recv()
            small_step(0)
        else:
            small_step(step - 1)
    small_step(steps - 1)
    value = own(0)
    for side in range(2):
        arrived[side].wait_recv()
        value = value + ring_in[(side + 1) * steps - 1].astype(F32)
    o_ref[...] = value
    value = own_small(0)
    for side in range(2):
        small_arrived[side].wait_recv()
        value = value + sm_in[(side + 1) * steps - 1]
    so_ref[...] = value
    for _, copy in pairs.values():
        copy.wait_send()
    sm_pair_copy.wait_send()
    for copy in sends:
        copy.wait_send()


def reduce_call(grad, small, chips, parts):
    rows, columns = grad.shape[2:]
    tile = small.shape[3:]
    sem = pltpu.SemaphoreType.DMA
    vmem = pl.BlockSpec(memory_space=pltpu.VMEM)
    return pl.pallas_call(
        functools.partial(reduce_kernel, chips, parts),
        out_shape=[
            jax.ShapeDtypeStruct((rows, columns), F32),
            jax.ShapeDtypeStruct(tile, F32),
        ],
        in_specs=[vmem, vmem],
        out_specs=[vmem, vmem],
        scratch_shapes=[
            pltpu.VMEM((chips, rows, columns), BF16),
            pltpu.VMEM((chips, rows, columns), BF16),
            pltpu.VMEM((chips, rows, columns), BF16),
            pltpu.VMEM((parts - 1, 2, chips) + tile, F32),
            pltpu.VMEM((2, chips) + tile, F32),
            pltpu.VMEM((chips,) + tile, F32),
            pltpu.VMEM((chips,) + tile, F32),
            pltpu.VMEM((chips,) + tile, F32),
        ]
        + [sem((chips,))] * 4
        + [sem((parts - 1,))] * 2
        + [sem((1,))] * 2
        + [sem((chips,))] * 2,
        compiler_params=pltpu.CompilerParams(
            collective_id=1, has_side_effects=True, vmem_limit_bytes=40 * 1024 * 1024
        ),
        cost_estimate=pl.CostEstimate(
            flops=0, bytes_accessed=64 * rows * columns, transcendentals=0
        ),
    )(grad, small)


def local(
    tokens,
    gain_one,
    shift_one,
    w_qkv,
    bias_qv,
    w_out,
    bias_out,
    gain_two,
    shift_two,
    w_up,
    bias_up,
    w_down,
    bias_down,
    cotangent,
):
    parts = lax.axis_size("tensor")
    n_dp = lax.axis_size("dp")
    everyone = n_dp * parts
    t_index = lax.axis_index("tensor")
    chips = n_dp // 2

    def gather_weight(shard):
        return lax.all_gather(shard, "dp", axis=0, tiled=True)

    def scatter_weight(grad):
        return lax.psum_scatter(grad, "dp", scatter_dimension=0, tiled=True).astype(F32)

    def gather_rows(mine):
        if parts == 2:
            return [mine, lax.ppermute(mine, "tensor", [(0, 1), (1, 0)])]
        return [lax.all_gather(mine, "tensor", axis=0, tiled=True)]

    def scatter_rows(product, blocks):
        if parts == 2:
            sent = lax.ppermute(product(blocks[1]).astype(BF16), "tensor", [(0, 1), (1, 0)])
            return product(blocks[0]) + sent.astype(F32)
        return lax.psum_scatter(
            product(blocks[0]).astype(BF16), "tensor", scatter_dimension=0, tiled=True
        ).astype(F32)

    def joined(blocks):
        return blocks[0] if len(blocks) == 1 else jnp.concatenate(blocks, axis=0)

    def split(rows):
        if parts == 2:
            return [rows[: rows.shape[0] // 2], rows[rows.shape[0] // 2 :]]
        return [rows]

    vec = gain_one.shape[0]
    n_qv = bias_qv.size
    n_bu = bias_up.size
    packed = jnp.concatenate(
        [gain_one, shift_one, bias_out, gain_two, shift_two, bias_down]
        + [bias_qv.astype(F32).reshape(-1), bias_up.astype(F32).reshape(-1)]
    )
    tile = (8, 128)
    pad = tile[0] * tile[1] - packed.size
    first_shard = jnp.concatenate([w_qkv[0], w_qkv[1], w_qkv[2], w_out.T], axis=1)
    first_full, small, other_tokens, other_cot = gather_call(
        first_shard, jnp.pad(packed, (0, pad)).reshape(tile), tokens, cotangent, chips, parts
    )
    first_full = first_full.reshape(-1, first_shard.shape[1])
    small = small.reshape(parts, n_dp, -1).transpose(1, 0, 2).reshape(everyone, -1)
    gain_a, shift_a, out_shift, gain_b, shift_b, down_shift = (
        small[:, n * vec : (n + 1) * vec].reshape(-1) for n in range(6)
    )
    at = 6 * vec
    end = at + n_qv + n_bu
    local_small = lax.dynamic_index_in_dim(
        small.reshape(n_dp, parts, -1), t_index, 1, keepdims=False
    )
    local_heads = bias_qv.shape[1]
    width = local_heads * HD
    qv_shift = (
        local_small[:, at : at + n_qv]
        .reshape(n_dp, 2, local_heads, -1)
        .transpose(1, 2, 0, 3)
        .reshape(2, width)
    )
    up_shift = (
        local_small[:, at + n_qv : end]
        .reshape(n_dp, bias_up.shape[0], -1)
        .transpose(1, 0, 2)
        .reshape(-1)
    )
    hidden_units = up_shift.shape[0]

    up_full = gather_weight(w_up)
    down_t = gather_weight(w_down.T)
    qkv_full = first_full[:, : 3 * width]
    out_t = first_full[:, 3 * width :]

    rows = tokens.shape[0]
    group = rows * parts
    length = min(SEQ_LEN, group)
    sequences = group // length
    head_ids = t_index * local_heads + lax.iota(jnp.int32, local_heads)
    slopes = jnp.exp2(-8.0 * (head_ids + 1).astype(F32) / H)
    flip = (t_index if parts == 2 else 0 * t_index).astype(jnp.int32).reshape(1)

    cot_blocks = [cotangent, other_cot] if parts == 2 else gather_rows(cotangent)
    inputs = tokens.astype(F32)
    normed_one, inverse_one = normalize(inputs)
    low_one = (normed_one * gain_a + shift_a).astype(BF16)
    if parts == 2:
        other_normed = normalize(other_tokens.astype(F32))[0]
        one_blocks = [low_one, (other_normed * gain_a + shift_a).astype(BF16)]
    else:
        one_blocks = gather_rows(low_one)
    qkv_shift = jnp.concatenate([qv_shift[0], jnp.zeros((width,), F32), qv_shift[1]])
    qkv_low = joined([(mm(b, qkv_full) + qkv_shift).astype(BF16) for b in one_blocks])
    query, keys, values = (qkv_low[:, n * width : (n + 1) * width] for n in range(3))
    pair_area = sequences * local_heads * length * length
    vmem = pltpu.VMEM((length, PAIR), BF16)
    (attended,) = attention_call(
        attend_kernel,
        flip,
        slopes,
        (query, keys, values),
        1,
        [vmem, vmem],
        length,
        pl.CostEstimate(
            flops=4 * PAIR * pair_area, bytes_accessed=8 * group * width, transcendentals=pair_area
        ),
    )
    middle = (
        inputs + scatter_rows(lambda b: mm_t(b, out_t), split(attended)) + out_shift
    )
    normed_two, inverse_two = normalize(middle)
    two_blocks = gather_rows((normed_two * gain_b + shift_b).astype(BF16))
    hidden = [mm(b, up_full) + up_shift for b in two_blocks]
    gated = [smooth_gate(h).astype(BF16) for h in hidden]
    grad_gated = [mm(c, down_t) for c in cot_blocks]
    grad_hidden = [
        jax.vjp(smooth_gate, h)[1](g)[0].astype(BF16) for h, g in zip(hidden, grad_gated)
    ]
    grad_two = scatter_rows(lambda b: mm_t(b, up_full), grad_hidden)

    cot_all = joined(cot_blocks)
    grad_hidden_all = joined(grad_hidden)
    summed_down = scatter_weight(t_mm(cot_all, joined(gated)).astype(BF16))
    summed_up = scatter_weight(t_mm(joined(two_blocks), grad_hidden_all).astype(BF16))
    grad_up_shift = jnp.sum(grad_hidden_all.astype(F32), axis=0)

    grad_out_rows = cotangent.astype(F32)
    grad_down_shift = jnp.sum(grad_out_rows, axis=0)
    grad_gain_b = jnp.sum(grad_two * normed_two, axis=0)
    grad_shift_b = jnp.sum(grad_two, axis=0)
    grad_middle = grad_out_rows + norm_backward(grad_two, normed_two, inverse_two, gain_b)
    grad_out_shift = jnp.sum(grad_middle, axis=0)
    low_blocks = gather_rows(grad_middle.astype(BF16))
    grad_attended = joined([mm(b, out_t).astype(BF16) for b in low_blocks])
    if parts == 2:
        late = lax.optimization_barrier((*gated, low_blocks[1]))[:2]
        away = mm_t(late[1], down_t).astype(BF16)
        grad_attended, away = lax.optimization_barrier((grad_attended, away))
        came = lax.ppermute(away, "tensor", [(0, 1), (1, 0)])
        feed = mm_t(late[0], down_t) + came.astype(F32)
    else:
        feed = scatter_rows(lambda b: mm_t(b, down_t), gated)
    output = middle + feed + down_shift
    scratch = [vmem, vmem] + [pltpu.VMEM((length, PAIR), F32)] * 2
    grad_qkv_parts = attention_call(
        attend_back_kernel,
        flip,
        slopes,
        (query, keys, values, grad_attended),
        3,
        scratch,
        length,
        pl.CostEstimate(
            flops=10 * PAIR * pair_area,
            bytes_accessed=14 * group * width,
            transcendentals=pair_area,
        ),
    )
    grad_qkv_rows = jnp.concatenate(grad_qkv_parts, axis=1)
    grad_one = scatter_rows(lambda b: mm_t(b, qkv_full), split(grad_qkv_rows))
    grad_first = jnp.concatenate(
        [
            t_mm(joined(one_blocks), grad_qkv_rows).astype(BF16),
            t_mm(joined(low_blocks), attended).astype(BF16),
        ],
        axis=1,
    )
    grad_qv_shift = jnp.stack(
        [
            jnp.sum(grad_qkv_parts[0].astype(F32), axis=0),
            jnp.sum(grad_qkv_parts[2].astype(F32), axis=0),
        ]
    )
    grad_gain_a = jnp.sum(grad_one * normed_one, axis=0)
    grad_shift_a = jnp.sum(grad_one, axis=0)
    grad_inputs = grad_middle + norm_backward(grad_one, normed_one, inverse_one, gain_a)

    mine = (lax.iota(jnp.int32, parts) == t_index)[None, :, None]

    def placed(values):
        return jnp.where(mine, values.reshape(n_dp, 1, -1), 0.0).reshape(everyone, -1)

    packed_grads = jnp.concatenate(
        [
            v.reshape(everyone, vec)
            for v in (
                grad_gain_a,
                grad_shift_a,
                grad_out_shift,
                grad_gain_b,
                grad_shift_b,
                grad_down_shift,
            )
        ]
        + [
            placed(grad_qv_shift.reshape(2, local_heads, n_dp, -1).transpose(2, 0, 1, 3)),
            placed(grad_up_shift.reshape(bias_up.shape[0], n_dp, -1).transpose(1, 0, 2)),
        ],
        axis=1,
    )
    packed_grads = (
        jnp.pad(packed_grads, ((0, 0), (0, pad)))
        .reshape((chips, 2, parts) + tile)
        .transpose(2, 1, 0, 3, 4)
    )
    output, summed_down, packed_grads = lax.optimization_barrier(
        (output.astype(BF16), summed_down.T, packed_grads)
    )
    summed_first, sums = reduce_call(
        grad_first.reshape(chips, 2, -1, grad_first.shape[1]), packed_grads, chips, parts
    )
    sums = sums.reshape(-1)
    sum_gain_a, sum_shift_a, sum_out_shift, sum_gain_b, sum_shift_b, sum_down_shift = (
        sums[n * vec : (n + 1) * vec] for n in range(6)
    )
    summed_qkv = jnp.stack([summed_first[:, n * width : (n + 1) * width] for n in range(3)])
    return (
        output,
        grad_inputs.astype(BF16),
        sum_gain_a,
        sum_shift_a,
        summed_qkv,
        sums[at : at + n_qv].reshape(bias_qv.shape),
        summed_first[:, 3 * width :].T,
        sum_out_shift,
        sum_gain_b,
        sum_shift_b,
        summed_up,
        sums[at + n_qv : end].reshape(bias_up.shape),
        summed_down,
        sum_down_shift,
    )


def solution(mesh):
    return jax.shard_map(
        local,
        mesh=mesh,
        in_specs=(
            P(("dp", "tensor"), None),
            P(("dp", "tensor")),
            P(("dp", "tensor")),
            P(None, "dp", "tensor"),
            P(None, "tensor", "dp"),
            P("tensor", "dp"),
            P(("dp", "tensor")),
            P(("dp", "tensor")),
            P(("dp", "tensor")),
            P("dp", "tensor"),
            P("tensor", "dp"),
            P("tensor", "dp"),
            P(("dp", "tensor")),
            P(("dp", "tensor"), None),
        ),
        out_specs=(
            P(("dp", "tensor"), None),
            P(("dp", "tensor"), None),
            P(("dp", "tensor")),
            P(("dp", "tensor")),
            P(None, "dp", "tensor"),
            P(None, "tensor", "dp"),
            P("tensor", "dp"),
            P(("dp", "tensor")),
            P(("dp", "tensor")),
            P(("dp", "tensor")),
            P("dp", "tensor"),
            P("tensor", "dp"),
            P("tensor", "dp"),
            P(("dp", "tensor")),
        ),
        check_vma=False,
    )
```
